128 devices in a mesh: grp: 4 (over x), sub: 32 (over y, z, core).
Axes of the slice: x: 4, y: 4, z: 4, core: 2. Of those that a mesh axis runs over, the one named last changes fastest.
Arguments:
- coordinates: bfloat16 [8192, 3, 256], P(('grp', 'sub')), may hold values from -1 to 1
- charges: bfloat16 [8192, 16, 256], P(('grp', 'sub')), may hold values from -6 to 6
- leaf_basis: bfloat16 [8192, 64, 256], P(('grp', 'sub')), may hold values from -0.375 to 0.375
- transfer: bfloat16 [8192, 64, 64], P(('grp', 'sub')), may hold values from -0.75 to 0.75
- skeleton: bfloat16 [1024, 3, 64], P(('grp', 'sub')), may hold values from -1 to 1
- send_plan: int32 [128, 128, 4], P(('grp', 'sub')), may hold values from 0 to 63
- near_lists: int32 [8192, 16], P(('grp', 'sub')), may hold values from 0 to 575
- near_count: int32 [8192], P(('grp', 'sub')), may hold values from 1 to 16, as said below
- far_lists: int32 [1024, 27], P(('grp', 'sub')), may hold values from 0 to 1023
Outputs:
- potential: bfloat16 [8192, 16, 256], P(('grp', 'sub'))
The draws below stay inside these ranges and needn't reach their ends.
Inputs may be any that keep to these rules, and one draw needn't show every extreme that they name: Entries of a leaf's neighbour list at positions near_count or later are ignored. Each device's leaves carry their own largest count; some device's largest is 16.
All inputs are finite; a program needn't handle non-finite values.
Results may differ from the reference program's by a relative error of at most 0.024.
Values may be sent and summed in bfloat16 or wider, within the bound.
No kernel may reach another device: no remote copies, remote signals or barrier semaphores. Data moves between devices by JAX's collectives and lax.ppermute only.
A program may use at most 64 MiB of HBM per device.

```python
import jax
import jax.numpy as jnp
from jax import lax

P_SIZE = 256
K = 64
R = 16
NEAR = 16
FARP = 27
CAP = 4
LEAF_DEV = 64
LEAVES = 8192
PARENTS = 1024
SLOTS = 576
N_GRP = 4
N_SUB = 32


def draw_near_count(key, part):
    key = jax.random.fold_in(key, 7)
    first, second, third = jax.random.split(key, 3)
    devices = N_GRP * N_SUB
    device_top = jax.random.randint(first, (devices,), 1, NEAR + 1)
    chosen = jax.random.randint(second, (), 0, devices)
    device_top = jnp.where(jnp.arange(devices) == chosen, NEAR, device_top)
    raw_draw = jax.random.randint(third, (devices, LEAF_DEV), 0, 1048576)
    counts = 1 + raw_draw % device_top[:, None]
    column_ids = jnp.arange(LEAF_DEV)[None, :]
    counts = jnp.where(column_ids == 0, device_top[:, None], counts)
    return counts.reshape(-1).astype(jnp.int32)


def touch_ends(entries, own_key, least, top_value):
    place = [jax.random.randint(jax.random.fold_in(own_key, axis), (), 0, length) for axis, length in enumerate(entries.shape)]
    widest = entries.shape.index(max(entries.shape))
    neighbour = place[:widest] + [(place[widest] + 1) % entries.shape[widest]] + place[widest + 1:]
    return entries.at[tuple(place)].set(least).at[tuple(neighbour)].set(top_value)


def block_levels(key, dims, cuts, least, largest):
    gain = 1.0
    for dim, blocks in cuts:
        steps = jax.random.uniform(jax.random.fold_in(jax.random.fold_in(key, 6), dim), (blocks,), jnp.float32, least / len(cuts), largest / len(cuts))
        gain = gain * jnp.repeat(jnp.exp(steps), dims[dim] // blocks).reshape((-1,) + (1,) * (len(dims) - 1 - dim))
    return gain


def noise(stream_key, dims, spread, reach, pieces=(), held_as=jnp.bfloat16):
    factor_of = block_levels(stream_key, dims, pieces, -0.22, 0.18) if pieces else 1.0
    drawn = jax.random.normal(stream_key, dims, jnp.float32) * spread * factor_of
    return jnp.minimum(jnp.maximum(drawn, -reach), reach).astype(held_as)


def setup_inputs(seed: int = 0) -> dict:
    keys = jax.random.split(jax.random.key(seed), 10)
    return {
        "coordinates": jnp.clip(jax.random.uniform(keys[0], (LEAVES, 3, P_SIZE), jnp.float32, -1.0, 1.0) * block_levels(keys[0], (LEAVES, 3, P_SIZE), ((0, 128),), -0.4, 0.0), -1.0, 1.0).astype(jnp.bfloat16),
        "charges": noise(keys[1], (LEAVES, R, P_SIZE), 1.0, 6.0, ((0, 128),)),
        "leaf_basis": noise(keys[2], (LEAVES, K, P_SIZE), P_SIZE ** -0.5, 0.375, ((0, 128),)),
        "transfer": noise(keys[3], (LEAVES, K, K), K ** -0.5, 0.75, ((0, 128),)),
        "skeleton": jnp.clip(jax.random.uniform(keys[4], (PARENTS, 3, K), jnp.float32, -1.0, 1.0) * block_levels(keys[4], (PARENTS, 3, K), ((0, 128),), -0.4, 0.0), -1.0, 1.0).astype(jnp.bfloat16),
        "send_plan": touch_ends(jax.random.randint(keys[5], (N_GRP * N_SUB, N_GRP * N_SUB, CAP), 0, LEAF_DEV), jax.random.fold_in(keys[5], 1), 0, LEAF_DEV - 1).astype(jnp.int32),
        "near_lists": touch_ends(jax.random.randint(keys[6], (LEAVES, NEAR), 0, SLOTS), jax.random.fold_in(keys[6], 1), 0, SLOTS - 1).astype(jnp.int32),
        "near_count": draw_near_count(jax.random.fold_in(keys[9], 71), 0),
        "far_lists": touch_ends(jax.random.randint(keys[8], (PARENTS, FARP), 0, PARENTS), jax.random.fold_in(keys[8], 1), 0, PARENTS - 1).astype(jnp.int32),
    }


SOFTENING = 0.01

def kernel_block(targets, sources):
    target_pos = targets.astype(jnp.float32)
    source_pos = sources.astype(jnp.float32)
    squared = jnp.zeros(source_pos.shape[:-2] + (source_pos.shape[-1], target_pos.shape[-1]), jnp.float32)
    for component in range(3):
        offset = source_pos[..., component, :, None] - target_pos[..., component, None, :]
        squared = squared + offset * offset
    return lax.rsqrt(squared + SOFTENING).astype(jnp.bfloat16)

def reference(coordinates, charges, leaf_basis, transfer, skeleton, send_plan, near_lists, near_count, far_lists):
    leaves = coordinates.shape[0]
    leaf_ids = jnp.arange(leaves, dtype=jnp.int32)
    owner_dev = leaf_ids // LEAF_DEV
    remote = jnp.maximum(near_lists - LEAF_DEV, 0)
    source_dev = remote // CAP
    source_slot = remote % CAP
    remote_leaf = source_dev * LEAF_DEV + send_plan[source_dev, owner_dev[:, None], source_slot]
    local_leaf = owner_dev[:, None] * LEAF_DEV + near_lists
    partners = jnp.where(near_lists < LEAF_DEV, local_leaf, remote_leaf).astype(jnp.int32)
    near_scale = float(P_SIZE * (NEAR + 1)) ** (-0.5)

    def leaf_block(block_index):
        leaf_rows = (block_index * LEAF_DEV + jnp.arange(LEAF_DEV, dtype=jnp.int32)).astype(jnp.int32)
        target = coordinates[leaf_rows]
        own = kernel_block(target, target)
        total = jnp.einsum('lrs,lst->lrt', charges[leaf_rows].astype(jnp.float32), own.astype(jnp.float32))
        for column in range(NEAR):
            source_rows = partners[leaf_rows, column]
            kernel_vals = kernel_block(target, coordinates[source_rows])
            block_term = jnp.einsum('lrs,lst->lrt', charges[source_rows].astype(jnp.float32), kernel_vals.astype(jnp.float32))
            is_live = (column < near_count[leaf_rows])[:, None, None]
            total = total + jnp.where(is_live, block_term, jnp.float32(0.0))
        return total
    near_sum = lax.map(leaf_block, jnp.arange(N_GRP * N_SUB, dtype=jnp.int32))
    near_sum = near_scale * near_sum.reshape(leaves, R, P_SIZE)
    moments = jnp.einsum('lkp,lrp->lrk', leaf_basis.astype(jnp.float32), charges.astype(jnp.float32)).astype(jnp.bfloat16)
    lifted = jnp.einsum('lrk,lkj->lrj', moments.astype(jnp.float32), transfer.astype(jnp.float32))
    parent_moments = lifted.reshape(leaves // 8, 8, R, K).sum(axis=1).astype(jnp.bfloat16)
    far_moments = parent_moments[far_lists]
    far_skeleton = skeleton[far_lists]
    couple = kernel_block(skeleton[:, None], far_skeleton)
    far_scale = float(FARP * K) ** (-0.5)
    local_coef = (far_scale * jnp.einsum('pfrs,pfst->prt', far_moments.astype(jnp.float32), couple.astype(jnp.float32))).astype(jnp.bfloat16)
    child_coef = jnp.einsum('lrj,lkj->lrk', local_coef[leaf_ids // 8].astype(jnp.float32), transfer.astype(jnp.float32)).astype(jnp.bfloat16)
    far_field = jnp.einsum('lrk,lkp->lrp', child_coef.astype(jnp.float32), leaf_basis.astype(jnp.float32))
    return (near_sum + far_field).astype(jnp.bfloat16)
```

```python
import functools

import jax
import jax.numpy as jnp
from jax import lax
from jax.experimental import pallas as pl
from jax.experimental.pallas import tpu as pltpu
from jax.sharding import PartitionSpec as P

SOFTENING = 0.01
AXES = ("grp", "sub")
BF16 = jnp.bfloat16
F32 = jnp.float32
I32 = jnp.int32
MIB = 1024 * 1024
GROUP = 8
UNROLL = 8

SMEM = pl.BlockSpec(memory_space=pltpu.SMEM)


def whole(shape):
    return pl.BlockSpec(shape, lambda *_: (0,) * len(shape))


def dot_nt(a, b):
    return lax.dot_general(a, b, (((1,), (1,)), ((), ())), preferred_element_type=F32)


def dot_nn(a, b):
    return lax.dot_general(a, b, (((1,), (0,)), ((), ())), preferred_element_type=F32)


def store_rows(table, comps):
    count = comps.shape[1]
    for k in range(8):
        for h in range(2):
            rows = jnp.zeros((count, 128), F32)
            if k % 4 < 3:
                rows = comps[k % 4, :, 128 * h : 128 * h + 128].astype(F32)
            table[h, pl.ds(k, count, stride=8), :] = rows


def pack_kernel(plan, comps, charges, out, table):
    step = pl.program_id(0)
    per_step = out.shape[0]

    @pl.when(step == 0)
    def _():
        store_rows(table, comps)

    first_half = lax.broadcasted_iota(I32, (8, 128), 0) < 4

    def one(e, _):
        rows = [plan[(step * per_step + e) * 4 + c] for c in range(4)]
        for c in range(4):
            out[e, 16 * c : 16 * c + 16, :] = charges[rows[c]]
        halves = []
        for h in range(2):
            pos = [table[h, pl.ds(pl.multiple_of(8 * r, 8), 8), :] for r in rows]
            low = jnp.where(first_half, pos[0], pos[1])
            high = jnp.where(first_half, pos[2], pos[3])
            halves.append(jnp.concatenate([low, high], axis=0))
        out[e, 64:80, :] = jnp.concatenate(halves, axis=1).astype(BF16)
        return 0

    lax.fori_loop(0, per_step, one, 0, unroll=4)


def pack(plan, comps, charges, devices):
    leaves, _, points = charges.shape
    per_step = 16
    return pl.pallas_call(
        pack_kernel,
        grid=(devices // per_step,),
        out_shape=jax.ShapeDtypeStruct((devices, 80, points), BF16),
        in_specs=[SMEM, whole(comps.shape), whole(charges.shape)],
        out_specs=pl.BlockSpec((per_step, 80, points), lambda i: (i, 0, 0)),
        scratch_shapes=[pltpu.VMEM((2, leaves * 8, 128), F32)],
        compiler_params=pltpu.CompilerParams(vmem_limit_bytes=24 * MIB),
        cost_estimate=pl.CostEstimate(flops=0, bytes_accessed=6 * MIB, transcendentals=0),
        name="pack",
    )(plan, comps, charges)


def moments_kernel(charges, basis, transfer, skel, out, table):
    def parent(p):
        total = jnp.zeros((16, 64), F32)
        for i in range(GROUP):
            leaf = p * GROUP + i
            moment = dot_nt(charges[leaf], basis[leaf]).astype(BF16)
            total = total + dot_nn(moment, transfer[leaf])
        return total

    def pair(a, _):
        both = jnp.concatenate([parent(a), parent(a + 4)], axis=1).astype(BF16)
        out[pl.ds(pl.multiple_of(16 * a, 16), 16), :] = both
        return 0

    lax.fori_loop(0, 4, pair, 0)
    table[...] = jnp.zeros_like(table)
    for k in range(3):
        rows = skel[k].astype(F32)
        table[pl.ds(k, 4, stride=4), :] = jnp.concatenate([rows[0:4], rows[4:8]], axis=1)
    out[64:80, :] = table[...].astype(BF16)


def parent_payload(charges, basis, transfer, skel):
    return pl.pallas_call(
        moments_kernel,
        out_shape=jax.ShapeDtypeStruct((80, 128), BF16),
        scratch_shapes=[pltpu.VMEM((16, 128), F32)],
        compiler_params=pltpu.CompilerParams(vmem_limit_bytes=24 * MIB),
        cost_estimate=pl.CostEstimate(flops=10**8, bytes_accessed=4 * MIB, transcendentals=0),
        name="moments",
    )(charges, basis, transfer, skel)


def near_blocks(items, base, steps, targets, row_of, charges_of, acc):
    def body(n, _):
        results = []
        for u in range(UNROLL):
            code = items[base + n * UNROLL + u]
            target = code >> 10
            source = code & 1023
            place = target & 7
            charge = charges_of(source)
            total = None
            for h in range(2):
                lanes = slice(128 * h, 128 * h + 128)
                tiles = []
                wide = []
                for k in range(3):
                    row = jnp.broadcast_to(row_of(h, source, k), (16, 128))
                    wide.append(jnp.concatenate([row, row], axis=1).astype(BF16))
                for q in range(8):
                    square = None
                    for k in range(3):
                        off = targets[place, k, 16 * q : 16 * q + 16, :] - wide[k]
                        square = off * off + BF16(SOFTENING) if k == 0 else square + off * off
                    tiles.append(lax.rsqrt(square))
                values = jnp.concatenate(tiles, axis=0)
                values = jnp.concatenate([values[:, :128], values[:, 128:]], axis=0)
                part = dot_nt(charge[:, lanes], values)
                total = part if total is None else total + part
            results.append((target, total))
        for target, total in results:
            acc[target] += total
        return 0

    lax.fori_loop(0, steps, body, 0)


GHOST_CAP = 8 * 16 + UNROLL


def local_kernel(
    lists, counts, comps, charges, targets, ghost_items, ghost_steps, near, table, acc, items
):
    step = pl.program_id(0)

    @pl.when(step == 0)
    def _():
        store_rows(table, comps)

    def leaf_entries(i, ends):
        local_end, ghost_end = ends
        leaf = step * GROUP + i
        live_count = counts[leaf]
        items[local_end] = i * 1024 + leaf
        local_end = local_end + 1
        for j in range(16):
            slot = lists[j * 64 + leaf]
            live = j < live_count
            is_local = slot < 64
            items[local_end] = i * 1024 + slot
            ghost_items[ghost_end] = i * 1024 + slot - 64
            local_end = local_end + jnp.where(live & is_local, 1, 0)
            ghost_end = ghost_end + jnp.where(live & jnp.logical_not(is_local), 1, 0)
        return local_end, ghost_end

    base = step * GHOST_CAP
    local_end, ghost_end = lax.fori_loop(0, GROUP, leaf_entries, (I32(0), base))
    for u in range(UNROLL):
        items[local_end + u] = 8 * 1024
        ghost_items[ghost_end + u] = 8 * 1024
    ghost_steps[step] = (ghost_end - base + UNROLL - 1) // UNROLL

    def spread(i, _):
        leaf = step * GROUP + i
        cols = [table[h, pl.ds(pl.multiple_of(8 * leaf, 8), 8), :].T for h in range(2)]
        for k in range(3):
            halves = [jnp.broadcast_to(cols[h][:, k : k + 1], (128, 128)) for h in range(2)]
            targets[i, k] = jnp.concatenate(halves, axis=1).astype(BF16)
        return 0

    lax.fori_loop(0, GROUP, spread, 0)

    acc[...] = jnp.zeros_like(acc)
    near_blocks(
        items,
        0,
        (local_end + UNROLL - 1) // UNROLL,
        targets,
        lambda h, s, k: table[h, pl.ds(8 * s + k, 1), :],
        lambda s: charges[s],
        acc,
    )
    near[...] = acc[0:GROUP]


def local_near(lists, counts, comps, charges):
    leaves, rhs, points = charges.shape
    groups = leaves // GROUP
    return pl.pallas_call(
        local_kernel,
        grid=(groups,),
        out_shape=(
            jax.ShapeDtypeStruct((leaves, 3, 128, points), BF16),
            jax.ShapeDtypeStruct((groups * GHOST_CAP,), I32),
            jax.ShapeDtypeStruct((groups,), I32),
            jax.ShapeDtypeStruct((leaves, rhs, points), F32),
        ),
        in_specs=[SMEM, SMEM, whole(comps.shape), whole(charges.shape)],
        out_specs=(
            pl.BlockSpec((GROUP, 3, 128, points), lambda i: (i, 0, 0, 0)),
            SMEM,
            SMEM,
            pl.BlockSpec((GROUP, rhs, points), lambda i: (i, 0, 0)),
        ),
        scratch_shapes=[
            pltpu.VMEM((2, leaves * 8, 128), F32),
            pltpu.VMEM((GROUP + 1, rhs, points), F32),
            pltpu.SMEM((8 * 17 + UNROLL,), I32),
        ],
        compiler_params=pltpu.CompilerParams(vmem_limit_bytes=32 * MIB),
        cost_estimate=pl.CostEstimate(
            flops=2 * 10**9, bytes_accessed=15 * MIB, transcendentals=8 * 10**6
        ),
        name="local_near",
    )(lists, counts, comps, charges)


def ghost_kernel(items, steps, ghosts, targets, start, near, table, acc):
    step = pl.program_id(0)

    @pl.when(step == 0)
    def _():
        def widen(e, _):
            rows = ghosts[e, 64:80, :].astype(F32)
            for h in range(2):
                table[h, pl.ds(pl.multiple_of(16 * e, 16), 16), :] = rows[:, 128 * h : 128 * h + 128]
            return 0

        lax.fori_loop(0, ghosts.shape[0], widen, 0, unroll=8)

    def charges_of(s):
        return ghosts[s >> 2, pl.ds(pl.multiple_of(16 * (s & 3), 16), 16), :]

    acc[0:GROUP] = start[...]
    acc[GROUP] = jnp.zeros(acc.shape[1:], F32)
    near_blocks(
        items,
        step * GHOST_CAP,
        steps[step],
        targets,
        lambda h, s, k: table[h, pl.ds(4 * s + k, 1), :],
        charges_of,
        acc,
    )
    near[...] = acc[0:GROUP]


def ghost_near(items, steps, ghosts, targets, start):
    leaves, rhs, points = start.shape
    devices = ghosts.shape[0]
    block = pl.BlockSpec((GROUP, rhs, points), lambda i: (i, 0, 0))
    return pl.pallas_call(
        ghost_kernel,
        grid=(leaves // GROUP,),
        out_shape=jax.ShapeDtypeStruct(start.shape, F32),
        in_specs=[
            SMEM,
            SMEM,
            whole(ghosts.shape),
            pl.BlockSpec((GROUP, 3, 128, points), lambda i: (i, 0, 0, 0)),
            block,
        ],
        out_specs=block,
        scratch_shapes=[
            pltpu.VMEM((2, devices * 16, 128), F32),
            pltpu.VMEM((GROUP + 1, rhs, points), F32),
        ],
        compiler_params=pltpu.CompilerParams(vmem_limit_bytes=40 * MIB),
        cost_estimate=pl.CostEstimate(
            flops=10**10, bytes_accessed=20 * MIB, transcendentals=4 * 10**7
        ),
        name="ghost_near",
    )(items, steps, ghosts, targets, start)


def finish_kernel(far, parents, skel, transfer, basis, near, out, table, own, *, scales):
    near_scale, far_scale = scales
    step = pl.program_id(0)

    @pl.when(step == 0)
    def _():
        def widen(e, _):
            table[pl.ds(pl.multiple_of(16 * e, 16), 16), :] = parents[e, 64:80, :].astype(F32)
            return 0

        lax.fori_loop(0, parents.shape[0], widen, 0, unroll=8)
        own[...] = jnp.zeros_like(own)
        for k in range(3):
            rows = skel[k].astype(F32)
            own[pl.ds(k, 8, stride=8), :] = jnp.concatenate([rows, rows], axis=1)

    cols = own[pl.ds(pl.multiple_of(8 * step, 8), 8), :].T
    target = [jnp.broadcast_to(cols[0:64, k : k + 1], (64, 128)) for k in range(3)]
    half = (lax.broadcasted_iota(I32, (16, 128), 1) >= 64).astype(I32)

    length = far.shape[0] // 8
    total = jnp.zeros((16, 64), F32)
    for f in range(length):
        parent = far[step * length + f]
        device, place = parent >> 3, parent & 7
        a, b = place & 3, place >> 2
        moment = parents[device, pl.ds(pl.multiple_of(16 * a, 16), 16), :]
        moment = jnp.where(half == b, moment.astype(F32), F32(0.0)).astype(BF16)
        square = None
        for k in range(3):
            off = target[k] - table[pl.ds(device * 16 + 4 * a + k, 1), :]
            square = off * off + SOFTENING if k == 0 else square + off * off
        total = total + dot_nt(moment, lax.rsqrt(square).astype(BF16))
    local = (far_scale * total).astype(BF16)
    for i in range(GROUP):
        child = dot_nt(local, transfer[i]).astype(BF16)
        out[i] = (near_scale * near[i] + dot_nn(child, basis[i])).astype(BF16)


def finish(far, parents, skel, transfer, basis, near, scales):
    leaves, rhs, points = near.shape
    groups = leaves // GROUP
    devices = parents.shape[0]

    def block(shape):
        return pl.BlockSpec((GROUP,) + shape[1:], lambda i: (i, 0, 0))

    return pl.pallas_call(
        functools.partial(finish_kernel, scales=scales),
        grid=(groups,),
        out_shape=jax.ShapeDtypeStruct(near.shape, BF16),
        in_specs=[
            SMEM,
            whole(parents.shape),
            whole(skel.shape),
            block(transfer.shape),
            block(basis.shape),
            block(near.shape),
        ],
        out_specs=block(near.shape),
        scratch_shapes=[pltpu.VMEM((devices * 16, 128), F32), pltpu.VMEM((64, 128), F32)],
        compiler_params=pltpu.CompilerParams(vmem_limit_bytes=24 * MIB),
        cost_estimate=pl.CostEstimate(
            flops=10**8, bytes_accessed=8 * MIB, transcendentals=10**6
        ),
        name="finish",
    )(far, parents, skel, transfer, basis, near)


def body(
    coordinates,
    charges,
    leaf_basis,
    transfer,
    skeleton,
    send_plan,
    near_lists,
    near_count,
    far_lists,
):
    points = charges.shape[2]
    rank = leaf_basis.shape[1]
    devices = send_plan.shape[1]
    scales = (
        float(points * (near_lists.shape[1] + 1)) ** (-0.5),
        float(far_lists.shape[1] * rank) ** (-0.5),
    )
    comps = jnp.transpose(coordinates, (1, 0, 2))
    skel = jnp.transpose(skeleton, (1, 0, 2))
    packed = pack(send_plan.reshape(-1), comps, charges, devices)
    ghosts = lax.all_to_all(packed, AXES, split_axis=0, concat_axis=0, tiled=True)
    payload = parent_payload(charges, leaf_basis, transfer, skel)
    parents = lax.all_gather(payload, AXES, axis=0, tiled=False)
    targets, items, steps, near = local_near(
        near_lists.T.reshape(-1), near_count, comps, charges
    )
    near = ghost_near(items, steps, ghosts, targets, near)
    return finish(far_lists.reshape(-1), parents, skel, transfer, leaf_basis, near, scales)


def solution(mesh):
    split3 = P(AXES, None, None)
    in_specs = (split3,) * 6 + (P(AXES, None), P(AXES), P(AXES, None))
    return jax.shard_map(body, mesh=mesh, in_specs=in_specs, out_specs=split3, check_vma=False)
```

```python
import functools

import jax
import jax.numpy as jnp
from jax import lax
from jax.experimental import pallas as pl
from jax.experimental.pallas import tpu as pltpu
from jax.sharding import PartitionSpec as P

SOFTENING = 0.01
AXES = ("grp", "sub")
BF16 = jnp.bfloat16
F32 = jnp.float32
I32 = jnp.int32
MIB = 1024 * 1024
VMEM_LIMIT = 60 * MIB
GROUP = 8
UNROLL = 16

SMEM = pl.BlockSpec(memory_space=pltpu.SMEM)
VMEM = pl.BlockSpec(memory_space=pltpu.VMEM)
HBM = pl.BlockSpec(memory_space=pltpu.HBM)


def fetch(source, target, semaphore):
    copy = pltpu.make_async_copy(source, target, semaphore)
    copy.start()
    return copy


def whole(shape):
    return pl.BlockSpec(shape, lambda *_: (0,) * len(shape))


def dot_nt(a, b):
    return lax.dot_general(a, b, (((1,), (1,)), ((), ())), preferred_element_type=F32)


def dot_nn(a, b):
    return lax.dot_general(a, b, (((1,), (0,)), ((), ())), preferred_element_type=F32)


def store_rows(table, comps):
    count = comps.shape[1]
    for k in range(8):
        for h in range(2):
            rows = jnp.zeros((count, 128), F32)
            if k % 4 < 3:
                rows = comps[k % 4, :, 128 * h : 128 * h + 128].astype(F32)
            table[h, pl.ds(k, count, stride=8), :] = rows


def pack_kernel(plan, comps_hbm, charges_hbm, out_hbm, comps, charges, table, out, sems):
    first = fetch(comps_hbm, comps, sems.at[0])
    second = fetch(charges_hbm, charges, sems.at[1])
    first.wait()
    store_rows(table, comps)
    second.wait()
    first_half = lax.broadcasted_iota(I32, (8, 128), 0) < 4

    def one(e, _):
        rows = [plan[c, e] for c in range(4)]
        for c in range(4):
            out[e, 16 * c : 16 * c + 16, :] = charges[rows[c]]
        halves = []
        for h in range(2):
            pos = [table[h, pl.ds(pl.multiple_of(8 * r, 8), 8), :] for r in rows]
            low = jnp.where(first_half, pos[0], pos[1])
            high = jnp.where(first_half, pos[2], pos[3])
            halves.append(jnp.concatenate([low, high], axis=0))
        out[e, 64:80, :] = jnp.concatenate(halves, axis=1).astype(BF16)
        return 0

    pieces = sems.shape[0] - 2
    size = out.shape[0] // pieces

    def piece(q):
        span = pl.ds(q * size, size)
        return pltpu.make_async_copy(out.at[span], out_hbm.at[span], sems.at[2 + q])

    for q in range(pieces):
        lax.fori_loop(q * size, (q + 1) * size, one, 0, unroll=4)
        piece(q).start()
    for q in range(pieces):
        piece(q).wait()


def pack(plan, comps, charges):
    leaves, _, points = charges.shape
    devices = plan.shape[1]
    return pl.pallas_call(
        pack_kernel,
        out_shape=jax.ShapeDtypeStruct((devices, 80, points), BF16),
        in_specs=[SMEM, HBM, HBM],
        out_specs=HBM,
        scratch_shapes=[
            pltpu.VMEM(comps.shape, BF16),
            pltpu.VMEM(charges.shape, BF16),
            pltpu.VMEM((2, leaves * 8, 128), F32),
            pltpu.VMEM((devices, 80, points), BF16),
            pltpu.SemaphoreType.DMA((2 + 4,)),
        ],
        compiler_params=pltpu.CompilerParams(vmem_limit_bytes=VMEM_LIMIT),
        cost_estimate=pl.CostEstimate(flops=0, bytes_accessed=6 * MIB, transcendentals=0),
        name="pack",
    )(plan, comps, charges)


def own_blocks():
    row = lax.broadcasted_iota(I32, (64, 256), 0) // 16
    return row == lax.broadcasted_iota(I32, (64, 256), 1) // 64


def moments_kernel(charges, basis, transfer, skel, copies, out, table):
    own = own_blocks()

    def parent(p):
        total = jnp.zeros((16, 64), F32)
        for quad in range(2):
            leaf = p * GROUP + 4 * quad
            sources = charges[pl.ds(leaf, 4)].reshape(64, 256)
            pairs = dot_nt(sources, basis[pl.ds(leaf, 4)].reshape(256, 256))
            pairs = jnp.where(own, pairs, F32(0.0))
            moment = pairs[0:16] + pairs[16:32] + pairs[32:48] + pairs[48:64]
            total = total + dot_nn(
                moment.astype(BF16), transfer[pl.ds(leaf, 4)].reshape(256, 64)
            )
        return total

    for a in range(4):
        both = jnp.concatenate([parent(a), parent(a + 4)], axis=1).astype(BF16)
        out[16 * a : 16 * a + 16, :] = both
    table[...] = jnp.zeros_like(table)
    for k in range(3):
        rows = skel[k].astype(F32)
        table[pl.ds(k, 4, stride=4), :] = jnp.concatenate([rows[0:4], rows[4:8]], axis=1)
    out[64:80, :] = table[...].astype(BF16)

    def copy(e, _):
        copies[e] = out[...]
        return 0

    lax.fori_loop(0, copies.shape[0], copy, 0, unroll=4)


def parent_payload(charges, basis, transfer, skel, devices):
    return pl.pallas_call(
        moments_kernel,
        out_shape=jax.ShapeDtypeStruct((devices, 80, 128), BF16),
        scratch_shapes=[pltpu.VMEM((80, 128), BF16), pltpu.VMEM((16, 128), F32)],
        compiler_params=pltpu.CompilerParams(vmem_limit_bytes=VMEM_LIMIT),
        cost_estimate=pl.CostEstimate(flops=10**8, bytes_accessed=4 * MIB, transcendentals=0),
        name="moments",
    )(charges, basis, transfer, skel)


def near_blocks(items, first, last, targets, row_of, charges_of, acc):
    def some(n, _):
        results = []
        for u in range(UNROLL):
            code = items[n * UNROLL + u]
            target = code >> 10
            source = code & 1023
            place = target & 63
            charge = charges_of(source)
            total = None
            for h in range(2):
                lanes = slice(128 * h, 128 * h + 128)
                tiles = []
                wide = []
                for k in range(3):
                    row = jnp.broadcast_to(row_of(h, source, k), (16, 128))
                    wide.append(jnp.concatenate([row, row], axis=1).astype(BF16))
                for q in range(8):
                    square = None
                    for k in range(3):
                        off = targets[place, k, 16 * q : 16 * q + 16, :] - wide[k]
                        square = off * off + BF16(SOFTENING) if k == 0 else square + off * off
                    tiles.append(lax.rsqrt(square))
                values = jnp.concatenate(tiles, axis=0)
                values = jnp.concatenate([values[:, :128], values[:, 128:]], axis=0)
                part = dot_nt(charge[:, lanes], values)
                total = part if total is None else total + part
            results.append((target, total))
        for target, total in results:
            acc[target] += total
        return 0

    lax.fori_loop(first, last, some, 0)


def local_kernel(
    lists, counts, comps, charges, targets, ghost_items, ghost_start, near, table, acc, items
):
    leaves = charges.shape[0]
    store_rows(table, comps)

    def leaf_entries(leaf, ends):
        local_end, ghost_end = ends
        ghost_start[leaf] = ghost_end
        live_count = counts[leaf]
        items[local_end] = leaf * 1024 + leaf
        local_end = local_end + 1
        for j in range(16):
            slot = lists[j, leaf]
            live = j < live_count
            is_local = slot < 64
            items[local_end] = leaf * 1024 + slot
            ghost_items[ghost_end] = leaf * 1024 + slot - 64
            local_end = local_end + jnp.where(live & is_local, 1, 0)
            ghost_end = ghost_end + jnp.where(live & jnp.logical_not(is_local), 1, 0)
        return local_end, ghost_end

    local_end, ghost_end = lax.fori_loop(0, leaves, leaf_entries, (I32(0), I32(0)))
    for u in range(UNROLL):
        items[local_end + u] = 64 * 1024
        ghost_items[ghost_end + u] = 64 * 1024
    ghost_start[leaves] = ghost_end

    def spread(leaf, _):
        cols = [table[h, pl.ds(pl.multiple_of(8 * leaf, 8), 8), :].T for h in range(2)]
        for k in range(3):
            halves = [jnp.broadcast_to(cols[h][:, k : k + 1], (128, 128)) for h in range(2)]
            targets[leaf, k] = jnp.concatenate(halves, axis=1).astype(BF16)
        return 0

    lax.fori_loop(0, leaves, spread, 0, unroll=2)

    acc[...] = jnp.zeros_like(acc)
    near_blocks(
        items,
        0,
        (local_end + UNROLL - 1) // UNROLL,
        targets,
        lambda h, s, k: table[h, pl.ds(8 * s + k, 1), :],
        lambda s: charges[s],
        acc,
    )
    near[...] = acc[0:leaves]


def local_near(lists, counts, comps, charges):
    leaves, rhs, points = charges.shape
    return pl.pallas_call(
        local_kernel,
        out_shape=(
            jax.ShapeDtypeStruct((leaves, 3, 128, points), BF16),
            jax.ShapeDtypeStruct((leaves * 16 + UNROLL,), I32),
            jax.ShapeDtypeStruct((leaves + 1,), I32),
            jax.ShapeDtypeStruct((leaves, rhs, points), F32),
        ),
        in_specs=[SMEM, SMEM, VMEM, VMEM],
        out_specs=(VMEM, SMEM, SMEM, VMEM),
        scratch_shapes=[
            pltpu.VMEM((2, leaves * 8, 128), F32),
            pltpu.VMEM((leaves + 1, rhs, points), F32),
            pltpu.SMEM((leaves * 17 + UNROLL,), I32),
        ],
        compiler_params=pltpu.CompilerParams(vmem_limit_bytes=VMEM_LIMIT),
        cost_estimate=pl.CostEstimate(
            flops=2 * 10**9, bytes_accessed=15 * MIB, transcendentals=8 * 10**6
        ),
        name="local_near",
    )(lists, counts, comps, charges)


PARTS = 4


def ghost_kernel(
    items, starts, ghosts, targets_hbm, start, near, targets, table, acc, sems
):
    leaves = start.shape[0]
    part = leaves // PARTS

    def piece(q):
        span = pl.ds(q * part, part)
        return pltpu.make_async_copy(targets_hbm.at[span], targets.at[span], sems.at[q])

    for q in range(PARTS):
        piece(q).start()

    def widen(e, _):
        rows = ghosts[e, 64:80, :].astype(F32)
        for h in range(2):
            table[h, pl.ds(pl.multiple_of(16 * e, 16), 16), :] = rows[:, 128 * h : 128 * h + 128]
        return 0

    lax.fori_loop(0, ghosts.shape[0], widen, 0, unroll=8)

    def charges_of(s):
        return ghosts[s >> 2, pl.ds(pl.multiple_of(16 * (s & 3), 16), 16), :]

    acc[0:leaves] = start[...]
    acc[leaves] = jnp.zeros(acc.shape[1:], F32)

    def run(q, _):
        piece(q).wait()
        end = starts[(q + 1) * part]
        last = jnp.where(q == PARTS - 1, (end + UNROLL - 1) // UNROLL, end // UNROLL)
        near_blocks(
            items,
            starts[q * part] // UNROLL,
            last,
            targets,
            lambda h, s, k: table[h, pl.ds(4 * s + k, 1), :],
            charges_of,
            acc,
        )
        return 0

    lax.fori_loop(0, PARTS, run, 0)
    near[...] = acc[0:leaves]


def ghost_near(items, starts, ghosts, targets, start):
    leaves, rhs, points = start.shape
    devices = ghosts.shape[0]
    return pl.pallas_call(
        ghost_kernel,
        out_shape=jax.ShapeDtypeStruct(start.shape, F32),
        in_specs=[SMEM, SMEM, VMEM, HBM, VMEM],
        out_specs=VMEM,
        scratch_shapes=[
            pltpu.VMEM(targets.shape, BF16),
            pltpu.VMEM((2, devices * 16, 128), F32),
            pltpu.VMEM((leaves + 1, rhs, points), F32),
            pltpu.SemaphoreType.DMA((PARTS,)),
        ],
        compiler_params=pltpu.CompilerParams(vmem_limit_bytes=VMEM_LIMIT),
        cost_estimate=pl.CostEstimate(
            flops=10**10, bytes_accessed=20 * MIB, transcendentals=4 * 10**7
        ),
        name="ghost_near",
    )(items, starts, ghosts, targets, start)


def finish_kernel(
    far,
    parents_hbm,
    skel,
    transfer_hbm,
    basis_hbm,
    near_hbm,
    out,
    parents,
    transfer,
    basis,
    near,
    table,
    own,
    local,
    sems,
    *,
    scales,
):
    near_scale, far_scale = scales
    clusters, length = far.shape
    fetches = [
        fetch(source, target, sems.at[n])
        for n, (source, target) in enumerate(
            [
                (parents_hbm, parents),
                (transfer_hbm, transfer),
                (basis_hbm, basis),
                (near_hbm, near),
            ]
        )
    ]
    fetches[0].wait()

    def widen(e, _):
        table[pl.ds(pl.multiple_of(16 * e, 16), 16), :] = parents[e, 64:80, :].astype(F32)
        return 0

    lax.fori_loop(0, parents.shape[0], widen, 0, unroll=8)
    own[...] = jnp.zeros_like(own)
    for k in range(3):
        rows = skel[k].astype(F32)
        own[pl.ds(k, clusters, stride=8), :] = jnp.concatenate([rows, rows], axis=1)

    half = (lax.broadcasted_iota(I32, (16, 128), 1) >= 64).astype(I32)

    def coefficients(p, _):
        cols = own[pl.ds(pl.multiple_of(8 * p, 8), 8), :].T
        target = [
            jnp.broadcast_to(cols[0:64, k : k + 1], (64, 128)).astype(BF16) for k in range(3)
        ]
        target = [jnp.concatenate([t, t], axis=1) for t in target]
        total = jnp.zeros((16, 64), F32)
        for first in range(0, length, 2):
            moments = []
            rows = [[], [], []]
            for f in (first, first + 1):
                parent = far[p, min(f, length - 1)]
                device, place = parent >> 3, parent & 7
                a, b = place & 3, place >> 2
                moment = parents[device, pl.ds(pl.multiple_of(16 * a, 16), 16), :]
                wanted = b if f < length else 2
                moments.append(jnp.where(half == wanted, moment.astype(F32), F32(0.0)))
                for k in range(3):
                    row = table[pl.ds(device * 16 + 4 * a + k, 1), :]
                    rows[k].append(jnp.broadcast_to(row, (16, 128)))
            rows = [jnp.concatenate(r, axis=1).astype(BF16) for r in rows]
            tiles = []
            for q in range(4):
                square = None
                for k in range(3):
                    off = target[k][16 * q : 16 * q + 16, :] - rows[k]
                    square = off * off + BF16(SOFTENING) if k == 0 else square + off * off
                tiles.append(lax.rsqrt(square))
            moment = jnp.concatenate(moments, axis=1).astype(BF16)
            total = total + dot_nt(moment, jnp.concatenate(tiles, axis=0))
        local[p] = (far_scale * total).astype(BF16)
        return 0

    lax.fori_loop(0, clusters, coefficients, 0)

    for copy in fetches[1:]:
        copy.wait()
    block = own_blocks()

    def leaves_of(p, _):
        coef = local[p]
        coef = jnp.concatenate([coef, coef, coef, coef], axis=0)
        for quad in range(2):
            leaf = p * GROUP + 4 * quad
            child = dot_nt(coef, transfer[pl.ds(leaf, 4)].reshape(256, 64))
            child = jnp.where(block, child, F32(0.0)).astype(BF16)
            field = dot_nn(child, basis[pl.ds(leaf, 4)].reshape(256, 256))
            total = near_scale * near[pl.ds(leaf, 4)] + field.reshape(4, 16, 256)
            out[pl.ds(leaf, 4)] = total.astype(BF16)
        return 0

    lax.fori_loop(0, clusters, leaves_of, 0, unroll=4)


def finish(far, parents, skel, transfer, basis, near, scales):
    devices = parents.shape[0]
    return pl.pallas_call(
        functools.partial(finish_kernel, scales=scales),
        out_shape=jax.ShapeDtypeStruct(near.shape, BF16),
        in_specs=[SMEM, HBM, VMEM, HBM, HBM, HBM],
        out_specs=VMEM,
        scratch_shapes=[
            pltpu.VMEM(parents.shape, BF16),
            pltpu.VMEM(transfer.shape, BF16),
            pltpu.VMEM(basis.shape, BF16),
            pltpu.VMEM(near.shape, F32),
            pltpu.VMEM((devices * 16, 128), F32),
            pltpu.VMEM((64, 128), F32),
            pltpu.VMEM((far.shape[0], 16, 64), BF16),
            pltpu.SemaphoreType.DMA((4,)),
        ],
        compiler_params=pltpu.CompilerParams(vmem_limit_bytes=VMEM_LIMIT),
        cost_estimate=pl.CostEstimate(
            flops=10**8, bytes_accessed=8 * MIB, transcendentals=10**6
        ),
        name="finish",
    )(far, parents, skel, transfer, basis, near)


def body(
    coordinates,
    charges,
    leaf_basis,
    transfer,
    skeleton,
    send_plan,
    near_lists,
    near_count,
    far_lists,
):
    points = charges.shape[2]
    rank = leaf_basis.shape[1]
    devices = send_plan.shape[1]
    scales = (
        float(points * (near_lists.shape[1] + 1)) ** (-0.5),
        float(far_lists.shape[1] * rank) ** (-0.5),
    )
    comps = jnp.transpose(coordinates, (1, 0, 2))
    skel = jnp.transpose(skeleton, (1, 0, 2))
    packed = pack(jnp.transpose(send_plan, (0, 2, 1))[0], comps, charges)
    ghosts = lax.all_to_all(packed, AXES, split_axis=0, concat_axis=0, tiled=True)
    payload = parent_payload(charges, leaf_basis, transfer, skel, devices)
    targets, items, starts, near = local_near(near_lists.T, near_count, comps, charges)
    payload, ghosts, near = lax.optimization_barrier((payload, ghosts, near))
    parents = lax.all_to_all(payload, AXES, split_axis=0, concat_axis=0, tiled=True)
    near = ghost_near(items, starts, ghosts, targets, near)
    return finish(far_lists, parents, skel, transfer, leaf_basis, near, scales)


def solution(mesh):
    split3 = P(AXES, None, None)
    in_specs = (split3,) * 6 + (P(AXES, None), P(AXES), P(AXES, None))
    return jax.shard_map(body, mesh=mesh, in_specs=in_specs, out_specs=split3, check_vma=False)
```

```python
import functools

import jax
import jax.numpy as jnp
from jax import lax
from jax.experimental import pallas as pl
from jax.experimental.pallas import tpu as pltpu
from jax.sharding import PartitionSpec as P

SOFTENING = 0.01
AXES = ("grp", "sub")
BF16 = jnp.bfloat16
F32 = jnp.float32
I32 = jnp.int32
MIB = 1024 * 1024
VMEM_LIMIT = 62 * MIB
GROUP = 8
UNROLL = 16

SMEM = pl.BlockSpec(memory_space=pltpu.SMEM)
VMEM = pl.BlockSpec(memory_space=pltpu.VMEM)
HBM = pl.BlockSpec(memory_space=pltpu.HBM)


def fetch(source, target, semaphore):
    copy = pltpu.make_async_copy(source, target, semaphore)
    copy.start()
    return copy


def whole(shape):
    return pl.BlockSpec(shape, lambda *_: (0,) * len(shape))


def dot_nt(a, b):
    return lax.dot_general(a, b, (((1,), (1,)), ((), ())), preferred_element_type=F32)


def dot_nn(a, b):
    return lax.dot_general(a, b, (((1,), (0,)), ((), ())), preferred_element_type=F32)


def store_rows(table, comps):
    count = comps.shape[1]
    for k in range(8):
        for h in range(2):
            rows = jnp.zeros((count, 128), F32)
            if k % 4 < 3:
                rows = comps[k % 4, :, 128 * h : 128 * h + 128].astype(F32)
            table[h, pl.ds(k, count, stride=8), :] = rows


def pack_kernel(plan, comps_hbm, charges_hbm, out_hbm, comps, charges, table, out, sems):
    first = fetch(comps_hbm, comps, sems.at[0])
    second = fetch(charges_hbm, charges, sems.at[1])
    first.wait()
    leaves = comps.shape[1]
    for t in range(3):
        for n in range(8):
            k, h = divmod((2 * t + n) % 6, 2)
            rows = comps[k, :, 128 * h : 128 * h + 128].astype(F32)
            table[t, pl.ds(n, leaves, stride=8), :] = rows
    second.wait()
    place = lax.broadcasted_iota(I32, (8, 128), 0)

    def one(e):
        rows = [plan[c, e] for c in range(4)]
        for c in range(4):
            for h in range(2):
                lanes = slice(128 * h, 128 * h + 128)
                first_row = 64 * h + 16 * c
                out[e, first_row : first_row + 16, :] = charges[rows[c], :, lanes]
        six = []
        for t, split in ((0, 6), (1, 4), (2, 2)):
            front = table[t, pl.ds(pl.multiple_of(8 * rows[t], 8), 8), :]
            back = table[t, pl.ds(pl.multiple_of(8 * rows[t + 1], 8), 8), :]
            six.append(jnp.where(place < split, front, back))
        out[e, 128:152, :] = jnp.concatenate(six, axis=0).astype(BF16)

    def four(e):
        for n in range(4):
            one(e + n)
        return 0

    pieces = sems.shape[0] - 2
    size = out.shape[0] // pieces

    def piece(q):
        span = pl.ds(q * size, size)
        return pltpu.make_async_copy(out.at[span], out_hbm.at[span], sems.at[2 + q])

    def some(q, _):
        lax.fori_loop(0, size // 4, lambda n, _: four(q * size + 4 * n), 0)
        piece(q).start()
        return 0

    lax.fori_loop(0, pieces, some, 0)
    for q in range(pieces):
        piece(q).wait()


def pack(plan, comps, charges):
    leaves = charges.shape[0]
    devices = plan.shape[1]
    return pl.pallas_call(
        pack_kernel,
        out_shape=jax.ShapeDtypeStruct((devices, 152, 128), BF16),
        in_specs=[SMEM, HBM, HBM],
        out_specs=HBM,
        scratch_shapes=[
            pltpu.VMEM(comps.shape, BF16),
            pltpu.VMEM(charges.shape, BF16),
            pltpu.VMEM((3, leaves * 8, 128), F32),
            pltpu.VMEM((devices, 152, 128), BF16),
            pltpu.SemaphoreType.DMA((2 + 8,)),
        ],
        compiler_params=pltpu.CompilerParams(vmem_limit_bytes=VMEM_LIMIT),
        cost_estimate=pl.CostEstimate(flops=0, bytes_accessed=6 * MIB, transcendentals=0),
        name="pack",
    )(plan, comps, charges)


def own_blocks():
    row = lax.broadcasted_iota(I32, (64, 256), 0) // 16
    return row == lax.broadcasted_iota(I32, (64, 256), 1) // 64


def moments_kernel(charges, basis, transfer, skel, copies, out, table):
    own = own_blocks()

    def parent(p):
        total = jnp.zeros((16, 64), F32)
        for quad in range(2):
            leaf = p * GROUP + 4 * quad
            sources = charges[pl.ds(leaf, 4)].reshape(64, 256)
            pairs = dot_nt(sources, basis[pl.ds(leaf, 4)].reshape(256, 256))
            pairs = jnp.where(own, pairs, F32(0.0))
            moment = pairs[0:16] + pairs[16:32] + pairs[32:48] + pairs[48:64]
            total = total + dot_nn(
                moment.astype(BF16), transfer[pl.ds(leaf, 4)].reshape(256, 64)
            )
        return total

    for a in range(4):
        both = jnp.concatenate([parent(a), parent(a + 4)], axis=1).astype(BF16)
        out[16 * a : 16 * a + 16, :] = both
    table[...] = jnp.zeros_like(table)
    for k in range(3):
        rows = skel[k].astype(F32)
        table[pl.ds(k, 4, stride=4), :] = jnp.concatenate([rows[0:4], rows[4:8]], axis=1)
    out[64:80, :] = table[...].astype(BF16)

    def copy(e, _):
        copies[e] = out[...]
        return 0

    lax.fori_loop(0, copies.shape[0], copy, 0, unroll=4)


def parent_payload(charges, basis, transfer, skel, devices):
    return pl.pallas_call(
        moments_kernel,
        out_shape=jax.ShapeDtypeStruct((devices, 80, 128), BF16),
        scratch_shapes=[pltpu.VMEM((80, 128), BF16), pltpu.VMEM((16, 128), F32)],
        compiler_params=pltpu.CompilerParams(vmem_limit_bytes=VMEM_LIMIT),
        cost_estimate=pl.CostEstimate(flops=10**8, bytes_accessed=4 * MIB, transcendentals=0),
        name="moments",
    )(charges, basis, transfer, skel)


def near_blocks(items, first, last, targets, row_of, charges_of, acc):
    def some(n, _):
        results = []
        for u in range(UNROLL):
            code = items[n * UNROLL + u]
            target = code >> 10
            source = code & 1023
            place = target & 63
            charge = charges_of(source)
            total = None
            for h in range(2):
                tiles = []
                wide = []
                for k in range(3):
                    row = jnp.broadcast_to(row_of(h, source, k), (16, 128))
                    wide.append(jnp.concatenate([row, row], axis=1).astype(BF16))
                for q in range(8):
                    square = None
                    for k in range(3):
                        off = targets[place, k, 16 * q : 16 * q + 16, :] - wide[k]
                        square = off * off + BF16(SOFTENING) if k == 0 else square + off * off
                    tiles.append(lax.rsqrt(square))
                values = jnp.concatenate(tiles, axis=0)
                values = jnp.concatenate([values[:, :128], values[:, 128:]], axis=0)
                part = dot_nt(charge[h], values)
                total = part if total is None else total + part
            results.append((target, total))
        for target, total in results:
            acc[target] += total
        return 0

    lax.fori_loop(first, last, some, 0)


def local_kernel(
    lists, counts, comps, charges, targets, ghost_items, ghost_start, near, table, acc, items
):
    leaves = charges.shape[0]
    store_rows(table, comps)

    def leaf_entries(leaf, ends):
        local_end, ghost_end = ends
        ghost_start[leaf] = ghost_end
        live_count = counts[leaf]
        items[local_end] = leaf * 1024 + leaf
        local_end = local_end + 1
        for j in range(16):
            slot = lists[j, leaf]
            live = j < live_count
            is_local = slot < 64
            items[local_end] = leaf * 1024 + slot
            ghost_items[ghost_end] = leaf * 1024 + slot - 64
            local_end = local_end + jnp.where(live & is_local, 1, 0)
            ghost_end = ghost_end + jnp.where(live & jnp.logical_not(is_local), 1, 0)
        return local_end, ghost_end

    local_end, ghost_end = lax.fori_loop(0, leaves, leaf_entries, (I32(0), I32(0)))
    for u in range(UNROLL):
        items[local_end + u] = 64 * 1024
        ghost_items[ghost_end + u] = 64 * 1024
    ghost_start[leaves] = ghost_end

    def spread(leaf, _):
        cols = [table[h, pl.ds(pl.multiple_of(8 * leaf, 8), 8), :].T for h in range(2)]
        for k in range(3):
            halves = [jnp.broadcast_to(cols[h][:, k : k + 1], (128, 128)) for h in range(2)]
            targets[leaf, k] = jnp.concatenate(halves, axis=1).astype(BF16)
        return 0

    lax.fori_loop(0, leaves, spread, 0, unroll=2)

    acc[...] = jnp.zeros_like(acc)
    near_blocks(
        items,
        0,
        (local_end + UNROLL - 1) // UNROLL,
        targets,
        lambda h, s, k: table[h, pl.ds(8 * s + k, 1), :],
        lambda s: [charges[s, :, 0:128], charges[s, :, 128:256]],
        acc,
    )
    near[...] = acc[0:leaves]


def local_near(lists, counts, comps, charges):
    leaves, rhs, points = charges.shape
    return pl.pallas_call(
        local_kernel,
        out_shape=(
            jax.ShapeDtypeStruct((leaves, 3, 128, points), BF16),
            jax.ShapeDtypeStruct((leaves * 16 + UNROLL,), I32),
            jax.ShapeDtypeStruct((leaves + 1,), I32),
            jax.ShapeDtypeStruct((leaves, rhs, points), F32),
        ),
        in_specs=[SMEM, SMEM, VMEM, VMEM],
        out_specs=(VMEM, SMEM, SMEM, VMEM),
        scratch_shapes=[
            pltpu.VMEM((2, leaves * 8, 128), F32),
            pltpu.VMEM((leaves + 1, rhs, points), F32),
            pltpu.SMEM((leaves * 17 + UNROLL,), I32),
        ],
        compiler_params=pltpu.CompilerParams(vmem_limit_bytes=VMEM_LIMIT),
        cost_estimate=pl.CostEstimate(
            flops=2 * 10**9, bytes_accessed=15 * MIB, transcendentals=8 * 10**6
        ),
        name="local_near",
    )(lists, counts, comps, charges)


PARTS = 4


def ghost_kernel(
    items, starts, ghosts_hbm, targets_hbm, start_hbm, near_hbm, ghosts, targets, table, acc, sems
):
    leaves = start_hbm.shape[0]
    part = leaves // PARTS
    senders = ghosts.shape[0] // PARTS

    def arrival(q):
        span = pl.ds(q * senders, senders)
        return pltpu.make_async_copy(ghosts_hbm.at[span], ghosts.at[span], sems.at[0, q])

    def piece(q):
        span = pl.ds(q * part, part)
        return pltpu.make_async_copy(targets_hbm.at[span], targets.at[span], sems.at[1, q])

    def result(q):
        span = pl.ds(q * part, part)
        return pltpu.make_async_copy(acc.at[span], near_hbm.at[span], sems.at[2, q])

    for q in range(PARTS):
        arrival(q).start()
    begin = fetch(start_hbm, acc.at[pl.ds(0, leaves)], sems.at[3, 0])
    for q in range(PARTS):
        piece(q).start()
    acc[leaves] = jnp.zeros(acc.shape[1:], F32)

    def widen(e, _):
        rows = ghosts[e, 128:152, :].astype(F32)
        table[pl.ds(pl.multiple_of(24 * e, 8), 24), :] = rows
        return 0

    def arrived(q, _):
        arrival(q).wait()
        lax.fori_loop(0, senders, lambda n, _: widen(q * senders + n, _), 0, unroll=8)
        return 0

    lax.fori_loop(0, PARTS, arrived, 0)
    begin.wait()

    def charges_of(s):
        return [
            ghosts[s >> 2, pl.ds(pl.multiple_of(64 * h + 16 * (s & 3), 16), 16), :]
            for h in range(2)
        ]

    def run(q, _):
        piece(q).wait()
        end = starts[(q + 1) * part]
        last = jnp.where(q == PARTS - 1, (end + UNROLL - 1) // UNROLL, end // UNROLL)
        near_blocks(
            items,
            starts[q * part] // UNROLL,
            last,
            targets,
            lambda h, s, k: table[pl.ds(6 * s + 2 * k + h, 1), :],
            charges_of,
            acc,
        )

        @pl.when(q > 0)
        def _():
            result(q - 1).start()

        return 0

    lax.fori_loop(0, PARTS, run, 0)
    result(PARTS - 1).start()
    for q in range(PARTS):
        result(q).wait()


def ghost_near(items, starts, ghosts, targets, start):
    leaves, rhs, points = start.shape
    devices = ghosts.shape[0]
    return pl.pallas_call(
        ghost_kernel,
        out_shape=jax.ShapeDtypeStruct(start.shape, F32),
        in_specs=[SMEM, SMEM, HBM, HBM, HBM],
        out_specs=HBM,
        scratch_shapes=[
            pltpu.VMEM(ghosts.shape, BF16),
            pltpu.VMEM(targets.shape, BF16),
            pltpu.VMEM((devices * 24, 128), F32),
            pltpu.VMEM((leaves + 1, rhs, points), F32),
            pltpu.SemaphoreType.DMA((4, PARTS)),
        ],
        compiler_params=pltpu.CompilerParams(vmem_limit_bytes=VMEM_LIMIT),
        cost_estimate=pl.CostEstimate(
            flops=10**10, bytes_accessed=20 * MIB, transcendentals=4 * 10**7
        ),
        name="ghost_near",
    )(items, starts, ghosts, targets, start)


def finish_kernel(
    far,
    parents,
    skel,
    transfer_hbm,
    basis_hbm,
    near_hbm,
    out,
    transfer,
    basis,
    near,
    table,
    own,
    local,
    sems,
    *,
    scales,
):
    near_scale, far_scale = scales
    clusters, length = far.shape
    fetches = [
        fetch(source, target, sems.at[n])
        for n, (source, target) in enumerate(
            [
                (transfer_hbm, transfer),
                (basis_hbm, basis),
                (near_hbm, near),
            ]
        )
    ]

    def widen(e, _):
        table[pl.ds(pl.multiple_of(16 * e, 16), 16), :] = parents[e, 64:80, :].astype(F32)
        return 0

    lax.fori_loop(0, parents.shape[0], widen, 0, unroll=8)
    own[...] = jnp.zeros_like(own)
    for k in range(3):
        rows = skel[k].astype(F32)
        own[pl.ds(k, clusters, stride=8), :] = jnp.concatenate([rows, rows], axis=1)

    half = (lax.broadcasted_iota(I32, (16, 128), 1) >= 64).astype(I32)

    def coefficients(p, _):
        cols = own[pl.ds(pl.multiple_of(8 * p, 8), 8), :].T
        target = [
            jnp.broadcast_to(cols[0:64, k : k + 1], (64, 128)).astype(BF16) for k in range(3)
        ]
        target = [jnp.concatenate([t, t], axis=1) for t in target]
        total = jnp.zeros((16, 64), F32)
        for first in range(0, length, 2):
            moments = []
            rows = [[], [], []]
            for f in (first, first + 1):
                parent = far[p, min(f, length - 1)]
                device, place = parent >> 3, parent & 7
                a, b = place & 3, place >> 2
                moment = parents[device, pl.ds(pl.multiple_of(16 * a, 16), 16), :]
                wanted = b if f < length else 2
                moments.append(jnp.where(half == wanted, moment.astype(F32), F32(0.0)))
                for k in range(3):
                    row = table[pl.ds(device * 16 + 4 * a + k, 1), :]
                    rows[k].append(jnp.broadcast_to(row, (16, 128)))
            rows = [jnp.concatenate(r, axis=1).astype(BF16) for r in rows]
            tiles = []
            for q in range(4):
                square = None
                for k in range(3):
                    off = target[k][16 * q : 16 * q + 16, :] - rows[k]
                    square = off * off + BF16(SOFTENING) if k == 0 else square + off * off
                tiles.append(lax.rsqrt(square))
            moment = jnp.concatenate(moments, axis=1).astype(BF16)
            total = total + dot_nt(moment, jnp.concatenate(tiles, axis=0))
        local[p] = (far_scale * total).astype(BF16)
        return 0

    lax.fori_loop(0, clusters, coefficients, 0, unroll=2)

    for copy in fetches:
        copy.wait()
    block = own_blocks()

    def leaves_of(p, _):
        coef = local[p]
        coef = jnp.concatenate([coef, coef, coef, coef], axis=0)
        for quad in range(2):
            leaf = p * GROUP + 4 * quad
            child = dot_nt(coef, transfer[pl.ds(leaf, 4)].reshape(256, 64))
            child = jnp.where(block, child, F32(0.0)).astype(BF16)
            field = dot_nn(child, basis[pl.ds(leaf, 4)].reshape(256, 256))
            total = near_scale * near[pl.ds(leaf, 4)] + field.reshape(4, 16, 256)
            out[pl.ds(leaf, 4)] = total.astype(BF16)
        return 0

    lax.fori_loop(0, clusters, leaves_of, 0, unroll=4)


def finish(far, parents, skel, transfer, basis, near, scales):
    devices = parents.shape[0]
    return pl.pallas_call(
        functools.partial(finish_kernel, scales=scales),
        out_shape=jax.ShapeDtypeStruct(near.shape, BF16),
        in_specs=[SMEM, VMEM, VMEM, HBM, HBM, HBM],
        out_specs=VMEM,
        scratch_shapes=[
            pltpu.VMEM(transfer.shape, BF16),
            pltpu.VMEM(basis.shape, BF16),
            pltpu.VMEM(near.shape, F32),
            pltpu.VMEM((devices * 16, 128), F32),
            pltpu.VMEM((64, 128), F32),
            pltpu.VMEM((far.shape[0], 16, 64), BF16),
            pltpu.SemaphoreType.DMA((3,)),
        ],
        compiler_params=pltpu.CompilerParams(vmem_limit_bytes=VMEM_LIMIT),
        cost_estimate=pl.CostEstimate(
            flops=10**8, bytes_accessed=8 * MIB, transcendentals=10**6
        ),
        name="finish",
    )(far, parents, skel, transfer, basis, near)


def body(
    coordinates,
    charges,
    leaf_basis,
    transfer,
    skeleton,
    send_plan,
    near_lists,
    near_count,
    far_lists,
):
    points = charges.shape[2]
    rank = leaf_basis.shape[1]
    devices = send_plan.shape[1]
    scales = (
        float(points * (near_lists.shape[1] + 1)) ** (-0.5),
        float(far_lists.shape[1] * rank) ** (-0.5),
    )
    comps = jnp.transpose(coordinates, (1, 0, 2))
    skel = jnp.transpose(skeleton, (1, 0, 2))
    packed = pack(jnp.transpose(send_plan, (0, 2, 1))[0], comps, charges)
    ghosts = lax.all_to_all(packed, AXES, split_axis=0, concat_axis=0, tiled=True)
    payload = parent_payload(charges, leaf_basis, transfer, skel, devices)
    targets, items, starts, near = local_near(near_lists.T, near_count, comps, charges)
    payload, ghosts, near = lax.optimization_barrier((payload, ghosts, near))
    parents = lax.all_to_all(payload, AXES, split_axis=0, concat_axis=0, tiled=True)
    near = ghost_near(items, starts, ghosts, targets, near)
    return finish(far_lists, parents, skel, transfer, leaf_basis, near, scales)


def solution(mesh):
    split3 = P(AXES, None, None)
    in_specs = (split3,) * 6 + (P(AXES, None), P(AXES), P(AXES, None))
    return jax.shard_map(body, mesh=mesh, in_specs=in_specs, out_specs=split3, check_vma=False)
```

```python
import functools

import jax
import jax.numpy as jnp
from jax import lax
from jax.experimental import pallas as pl
from jax.experimental.pallas import tpu as pltpu
from jax.sharding import Mesh
from jax.sharding import PartitionSpec as P

SOFTENING = 0.01
AXES = ("x", "y", "z", "core")
RING = 4
BF16 = jnp.bfloat16
F32 = jnp.float32
I32 = jnp.int32
MIB = 1024 * 1024
VMEM_LIMIT = 62 * MIB
GROUP = 8
UNROLL = 16

SMEM = pl.BlockSpec(memory_space=pltpu.SMEM)
VMEM = pl.BlockSpec(memory_space=pltpu.VMEM)
HBM = pl.BlockSpec(memory_space=pltpu.HBM)


def fetch(source, target, semaphore):
    copy = pltpu.make_async_copy(source, target, semaphore)
    copy.start()
    return copy


def whole(shape):
    return pl.BlockSpec(shape, lambda *_: (0,) * len(shape))


def dot_nt(a, b):
    return lax.dot_general(a, b, (((1,), (1,)), ((), ())), preferred_element_type=F32)


def dot_nn(a, b):
    return lax.dot_general(a, b, (((1,), (0,)), ((), ())), preferred_element_type=F32)


def store_rows(table, comps):
    count = comps.shape[1]
    for k in range(8):
        for h in range(2):
            rows = jnp.zeros((count, 128), F32)
            if k % 4 < 3:
                rows = comps[k % 4, :, 128 * h : 128 * h + 128].astype(F32)
            table[h, pl.ds(k, count, stride=8), :] = rows


def pack_kernel(
    plan_hbm, comps_hbm, charges_hbm, out_hbm, comps, charges, table, out, plan, sems
):
    first = fetch(comps_hbm, comps, sems.at[0])
    second = fetch(charges_hbm, charges, sems.at[1])
    third = fetch(plan_hbm, plan, sems.at[2])
    first.wait()
    leaves = comps.shape[1]
    for t in range(3):
        for n in range(8):
            k, h = divmod((2 * t + n) % 6, 2)
            rows = comps[k, :, 128 * h : 128 * h + 128].astype(F32)
            table[t, pl.ds(n, leaves, stride=8), :] = rows
    second.wait()
    third.wait()
    place = lax.broadcasted_iota(I32, (8, 128), 0)

    def one(e):
        rows = [plan[c, e] for c in range(4)]
        for c in range(4):
            for h in range(2):
                lanes = slice(128 * h, 128 * h + 128)
                first_row = 64 * h + 16 * c
                out[e, first_row : first_row + 16, :] = charges[rows[c], :, lanes]
        six = []
        for t, split in ((0, 6), (1, 4), (2, 2)):
            front = table[t, pl.ds(pl.multiple_of(8 * rows[t], 8), 8), :]
            back = table[t, pl.ds(pl.multiple_of(8 * rows[t + 1], 8), 8), :]
            six.append(jnp.where(place < split, front, back))
        out[e, 128:152, :] = jnp.concatenate(six, axis=0).astype(BF16)

    def four(e):
        for n in range(4):
            one(e + n)
        return 0

    pieces = sems.shape[0] - 3
    size = out.shape[0] // pieces

    def piece(q):
        span = pl.ds(q * size, size)
        return pltpu.make_async_copy(out.at[span], out_hbm.at[span], sems.at[3 + q])

    def some(q, _):
        lax.fori_loop(0, size // 4, lambda n, _: four(q * size + 4 * n), 0)
        piece(q).start()
        return 0

    lax.fori_loop(0, pieces, some, 0)
    for q in range(pieces):
        piece(q).wait()


def pack(plan, comps, charges):
    leaves = charges.shape[0]
    devices = plan.shape[1]
    return pl.pallas_call(
        pack_kernel,
        out_shape=jax.ShapeDtypeStruct((devices, 152, 128), BF16),
        in_specs=[HBM, HBM, HBM],
        out_specs=HBM,
        scratch_shapes=[
            pltpu.VMEM(comps.shape, BF16),
            pltpu.VMEM(charges.shape, BF16),
            pltpu.VMEM((3, leaves * 8, 128), F32),
            pltpu.VMEM((devices, 152, 128), BF16),
            pltpu.SMEM(plan.shape, I32),
            pltpu.SemaphoreType.DMA((3 + 8,)),
        ],
        compiler_params=pltpu.CompilerParams(vmem_limit_bytes=VMEM_LIMIT),
        cost_estimate=pl.CostEstimate(flops=0, bytes_accessed=6 * MIB, transcendentals=0),
        name="pack",
    )(plan, comps, charges)


def own_blocks():
    row = lax.broadcasted_iota(I32, (64, 256), 0) // 16
    return row == lax.broadcasted_iota(I32, (64, 256), 1) // 64


def moments_kernel(charges, basis, transfer, skel, out, table):
    own = own_blocks()

    def parent(p):
        total = jnp.zeros((16, 64), F32)
        for quad in range(2):
            leaf = p * GROUP + 4 * quad
            sources = charges[pl.ds(leaf, 4)].reshape(64, 256)
            pairs = dot_nt(sources, basis[pl.ds(leaf, 4)].reshape(256, 256))
            pairs = jnp.where(own, pairs, F32(0.0))
            moment = pairs[0:16] + pairs[16:32] + pairs[32:48] + pairs[48:64]
            total = total + dot_nn(
                moment.astype(BF16), transfer[pl.ds(leaf, 4)].reshape(256, 64)
            )
        return total

    for a in range(4):
        both = jnp.concatenate([parent(a), parent(a + 4)], axis=1).astype(BF16)
        out[16 * a : 16 * a + 16, :] = both
    table[...] = jnp.zeros_like(table)
    for k in range(3):
        rows = skel[k].astype(F32)
        table[pl.ds(k, 4, stride=3), :] = jnp.concatenate([rows[0:4], rows[4:8]], axis=1)
    out[64:80, :] = table[...].astype(BF16)


def parent_payload(charges, basis, transfer, skel):
    return pl.pallas_call(
        moments_kernel,
        out_shape=jax.ShapeDtypeStruct((80, 128), BF16),
        scratch_shapes=[pltpu.VMEM((16, 128), F32)],
        compiler_params=pltpu.CompilerParams(vmem_limit_bytes=VMEM_LIMIT),
        cost_estimate=pl.CostEstimate(flops=10**8, bytes_accessed=4 * MIB, transcendentals=0),
        name="moments",
    )(charges, basis, transfer, skel)


def ring_kernel(*refs):
    pieces, (out, rows, held, sems) = refs[:-4], refs[-4:]
    for t, piece in enumerate(pieces):
        held[64 * t : 64 * t + 64, :] = piece[0:64, :]
        rows[12 * t : 12 * t + 16, :] = piece[64:80, :].astype(F32)
    held[256:304, :] = rows[0:48, :].astype(BF16)
    leaving = [fetch(held, out.at[g], sems.at[g]) for g in range(out.shape[0])]
    for copy in leaving:
        copy.wait()


def ring_copies(payload, groups):
    pieces = [payload]
    for dx in range(1, RING):
        pieces.append(lax.ppermute(payload, "x", [(x, (x + dx) % RING) for x in range(RING)]))
    lanes = payload.shape[1]
    return pl.pallas_call(
        ring_kernel,
        out_shape=jax.ShapeDtypeStruct((groups, 304, lanes), BF16),
        in_specs=[VMEM] * RING,
        out_specs=HBM,
        scratch_shapes=[
            pltpu.VMEM((64, lanes), F32),
            pltpu.VMEM((304, lanes), BF16),
            pltpu.SemaphoreType.DMA((groups,)),
        ],
        compiler_params=pltpu.CompilerParams(vmem_limit_bytes=VMEM_LIMIT),
        cost_estimate=pl.CostEstimate(flops=0, bytes_accessed=3 * MIB, transcendentals=0),
        name="ring_copies",
    )(*pieces)


def near_blocks(items, first, last, targets, row_of, charges_of, acc):
    def some(n, _):
        results = []
        for u in range(UNROLL):
            code = items[n * UNROLL + u]
            target = code >> 10
            source = code & 1023
            place = target & 63
            charge = charges_of(source)
            total = None
            for h in range(2):
                tiles = []
                wide = []
                for k in range(3):
                    row = jnp.broadcast_to(row_of(h, source, k), (16, 128))
                    wide.append(jnp.concatenate([row, row], axis=1).astype(BF16))
                for q in range(8):
                    square = None
                    for k in range(3):
                        off = targets[place, k, 16 * q : 16 * q + 16, :] - wide[k]
                        square = off * off + BF16(SOFTENING) if k == 0 else square + off * off
                    tiles.append(lax.rsqrt(square))
                values = jnp.concatenate(tiles, axis=0)
                values = jnp.concatenate([values[:, :128], values[:, 128:]], axis=0)
                part = dot_nt(charge[h], values)
                total = part if total is None else total + part
            results.append((target, total))
        for target, total in results:
            acc[target] += total
        return 0

    lax.fori_loop(first, last, some, 0)


def local_kernel(
    lists, counts, comps, charges, targets, ghost_items, ghost_start, near, table, acc, items
):
    leaves = charges.shape[0]
    store_rows(table, comps)

    def leaf_entries(leaf, ends):
        local_end, ghost_end = ends
        ghost_start[leaf] = ghost_end
        live_count = counts[leaf]
        items[local_end] = leaf * 1024 + leaf
        local_end = local_end + 1
        for j in range(16):
            slot = lists[j, leaf]
            live = j < live_count
            is_local = slot < 64
            items[local_end] = leaf * 1024 + slot
            ghost_items[ghost_end] = leaf * 1024 + slot - 64
            local_end = local_end + jnp.where(live & is_local, 1, 0)
            ghost_end = ghost_end + jnp.where(live & jnp.logical_not(is_local), 1, 0)
        return local_end, ghost_end

    local_end, ghost_end = lax.fori_loop(0, leaves, leaf_entries, (I32(0), I32(0)))
    for u in range(UNROLL):
        items[local_end + u] = 64 * 1024
        ghost_items[ghost_end + u] = 64 * 1024
    ghost_start[leaves] = ghost_end

    def spread(leaf, _):
        cols = [table[h, pl.ds(pl.multiple_of(8 * leaf, 8), 8), :].T for h in range(2)]
        for k in range(3):
            halves = [jnp.broadcast_to(cols[h][:, k : k + 1], (128, 128)) for h in range(2)]
            targets[leaf, k] = jnp.concatenate(halves, axis=1).astype(BF16)
        return 0

    lax.fori_loop(0, leaves, spread, 0, unroll=2)

    acc[...] = jnp.zeros_like(acc)
    near_blocks(
        items,
        0,
        (local_end + UNROLL - 1) // UNROLL,
        targets,
        lambda h, s, k: table[h, pl.ds(8 * s + k, 1), :],
        lambda s: [charges[s, :, 0:128], charges[s, :, 128:256]],
        acc,
    )
    near[...] = acc[0:leaves]


def local_near(lists, counts, comps, charges):
    leaves, rhs, points = charges.shape
    return pl.pallas_call(
        local_kernel,
        out_shape=(
            jax.ShapeDtypeStruct((leaves, 3, 128, points), BF16),
            jax.ShapeDtypeStruct((leaves * 16 + UNROLL,), I32),
            jax.ShapeDtypeStruct((leaves + 1,), I32),
            jax.ShapeDtypeStruct((leaves, rhs, points), F32),
        ),
        in_specs=[SMEM, SMEM, VMEM, VMEM],
        out_specs=(VMEM, SMEM, SMEM, VMEM),
        scratch_shapes=[
            pltpu.VMEM((2, leaves * 8, 128), F32),
            pltpu.VMEM((leaves + 1, rhs, points), F32),
            pltpu.SMEM((leaves * 17 + UNROLL,), I32),
        ],
        compiler_params=pltpu.CompilerParams(vmem_limit_bytes=VMEM_LIMIT),
        cost_estimate=pl.CostEstimate(
            flops=2 * 10**9, bytes_accessed=15 * MIB, transcendentals=8 * 10**6
        ),
        name="local_near",
    )(lists, counts, comps, charges)


PARTS = 4


def ghost_kernel(
    items, starts, ghosts_hbm, targets_hbm, start_hbm, near_hbm, ghosts, targets, table, acc, sems
):
    leaves = start_hbm.shape[0]
    part = leaves // PARTS
    senders = ghosts.shape[0] // PARTS

    def arrival(q):
        span = pl.ds(q * senders, senders)
        return pltpu.make_async_copy(ghosts_hbm.at[span], ghosts.at[span], sems.at[0, q])

    def piece(q):
        span = pl.ds(q * part, part)
        return pltpu.make_async_copy(targets_hbm.at[span], targets.at[span], sems.at[1, q])

    def result(q):
        span = pl.ds(q * part, part)
        return pltpu.make_async_copy(acc.at[span], near_hbm.at[span], sems.at[2, q])

    for q in range(PARTS):
        arrival(q).start()
    begin = fetch(start_hbm, acc.at[pl.ds(0, leaves)], sems.at[3, 0])
    piece(0).start()
    acc[leaves] = jnp.zeros(acc.shape[1:], F32)

    def widen(e, _):
        rows = ghosts[e, 128:152, :].astype(F32)
        table[pl.ds(pl.multiple_of(24 * e, 8), 24), :] = rows
        return 0

    def arrived(q, _):
        arrival(q).wait()
        lax.fori_loop(0, senders, lambda n, _: widen(q * senders + n, _), 0, unroll=8)
        return 0

    lax.fori_loop(0, PARTS, arrived, 0)
    begin.wait()
    for q in range(1, PARTS):
        piece(q).start()

    def charges_of(s):
        return [
            ghosts[s >> 2, pl.ds(pl.multiple_of(64 * h + 16 * (s & 3), 16), 16), :]
            for h in range(2)
        ]

    def run(q, _):
        piece(q).wait()
        end = starts[(q + 1) * part]
        last = jnp.where(q == PARTS - 1, (end + UNROLL - 1) // UNROLL, end // UNROLL)
        near_blocks(
            items,
            starts[q * part] // UNROLL,
            last,
            targets,
            lambda h, s, k: table[pl.ds(6 * s + 2 * k + h, 1), :],
            charges_of,
            acc,
        )
        return 0

    lax.fori_loop(0, PARTS, run, 0)
    for q in range(PARTS):
        result(q).start()
    for q in range(PARTS):
        result(q).wait()


def ghost_near(items, starts, ghosts, targets, start):
    leaves, rhs, points = start.shape
    devices = ghosts.shape[0]
    return pl.pallas_call(
        ghost_kernel,
        out_shape=jax.ShapeDtypeStruct(start.shape, F32),
        in_specs=[SMEM, SMEM, HBM, HBM, HBM],
        out_specs=HBM,
        scratch_shapes=[
            pltpu.VMEM(ghosts.shape, BF16),
            pltpu.VMEM(targets.shape, BF16),
            pltpu.VMEM((devices * 24, 128), F32),
            pltpu.VMEM((leaves + 1, rhs, points), F32),
            pltpu.SemaphoreType.DMA((4, PARTS)),
        ],
        compiler_params=pltpu.CompilerParams(vmem_limit_bytes=VMEM_LIMIT),
        cost_estimate=pl.CostEstimate(
            flops=10**10, bytes_accessed=20 * MIB, transcendentals=4 * 10**7
        ),
        name="ghost_near",
    )(items, starts, ghosts, targets, start)


def finish_kernel(
    far,
    parents,
    skel,
    transfer_hbm,
    basis_hbm,
    near_hbm,
    out_hbm,
    out,
    transfer,
    basis,
    near,
    table,
    own,
    local,
    sems,
    *,
    scales,
):
    near_scale, far_scale = scales
    clusters, length = far.shape
    fetches = [
        fetch(source, target, sems.at[n])
        for n, (source, target) in enumerate(
            [
                (transfer_hbm, transfer),
                (basis_hbm, basis),
                (near_hbm, near),
            ]
        )
    ]

    def widen(e, _):
        table[pl.ds(pl.multiple_of(48 * e, 16), 48), :] = parents[e, 256:304, :].astype(F32)
        return 0

    lax.fori_loop(0, parents.shape[0], widen, 0, unroll=4)
    own[...] = jnp.zeros_like(own)
    for k in range(3):
        rows = skel[k].astype(F32)
        own[pl.ds(k, clusters, stride=8), :] = jnp.concatenate([rows, rows], axis=1)

    half = (lax.broadcasted_iota(I32, (16, 128), 1) >= 64).astype(I32)

    def coefficients(p, _):
        cols = own[pl.ds(pl.multiple_of(8 * p, 8), 8), :].T
        target = [
            jnp.broadcast_to(cols[0:64, k : k + 1], (64, 128)).astype(BF16) for k in range(3)
        ]
        target = [jnp.concatenate([t, t], axis=1) for t in target]
        total = jnp.zeros((16, 64), F32)
        for first in range(0, length, 2):
            moments = []
            rows = [[], [], []]
            for f in (first, first + 1):
                code = far[p, min(f, length - 1)]
                group, inner, wanted = code >> 8, code & 15, (code >> 4) & 1
                wanted = wanted if f < length else 2
                moment = parents[group, pl.ds(pl.multiple_of(16 * inner, 16), 16), :]
                moments.append(jnp.where(half == wanted, moment.astype(F32), F32(0.0)))
                for k in range(3):
                    row = table[pl.ds(48 * group + 3 * inner + k, 1), :]
                    rows[k].append(jnp.broadcast_to(row, (16, 128)))
            rows = [jnp.concatenate(r, axis=1).astype(BF16) for r in rows]
            tiles = []
            for q in range(4):
                square = None
                for k in range(3):
                    off = target[k][16 * q : 16 * q + 16, :] - rows[k]
                    square = off * off + BF16(SOFTENING) if k == 0 else square + off * off
                tiles.append(lax.rsqrt(square))
            moment = jnp.concatenate(moments, axis=1).astype(BF16)
            total = total + dot_nt(moment, jnp.concatenate(tiles, axis=0))
        local[p] = (far_scale * total).astype(BF16)
        return 0

    lax.fori_loop(0, clusters, coefficients, 0, unroll=2)

    for copy in fetches:
        copy.wait()
    block = own_blocks()

    def leaves_of(p):
        coef = local[p]
        coef = jnp.concatenate([coef, coef, coef, coef], axis=0)
        for quad in range(2):
            leaf = p * GROUP + 4 * quad
            child = dot_nt(coef, transfer[pl.ds(leaf, 4)].reshape(256, 64))
            child = jnp.where(block, child, F32(0.0)).astype(BF16)
            field = dot_nn(child, basis[pl.ds(leaf, 4)].reshape(256, 256))
            total = near_scale * near[pl.ds(leaf, 4)] + field.reshape(4, 16, 256)
            out[pl.ds(leaf, 4)] = total.astype(BF16)

    def half_of(n):
        span = pl.ds(n * 4 * GROUP, 4 * GROUP)
        return pltpu.make_async_copy(out.at[span], out_hbm.at[span], sems.at[3 + n])

    def half_leaves(n, _):
        for p in range(4):
            leaves_of(4 * n + p)
        half_of(n).start()
        return 0

    lax.fori_loop(0, 2, half_leaves, 0)
    for n in range(2):
        half_of(n).wait()


def finish(far, parents, skel, transfer, basis, near, scales):
    devices = parents.shape[0] * RING
    return pl.pallas_call(
        functools.partial(finish_kernel, scales=scales),
        out_shape=jax.ShapeDtypeStruct(near.shape, BF16),
        in_specs=[SMEM, VMEM, VMEM, HBM, HBM, HBM],
        out_specs=HBM,
        scratch_shapes=[
            pltpu.VMEM(near.shape, BF16),
            pltpu.VMEM(transfer.shape, BF16),
            pltpu.VMEM(basis.shape, BF16),
            pltpu.VMEM(near.shape, F32),
            pltpu.VMEM((devices * 12, 128), F32),
            pltpu.VMEM((64, 128), F32),
            pltpu.VMEM((far.shape[0], 16, 64), BF16),
            pltpu.SemaphoreType.DMA((3 + 2,)),
        ],
        compiler_params=pltpu.CompilerParams(vmem_limit_bytes=VMEM_LIMIT),
        cost_estimate=pl.CostEstimate(
            flops=10**8, bytes_accessed=8 * MIB, transcendentals=10**6
        ),
        name="finish",
    )(far, parents, skel, transfer, basis, near)


def body(
    coordinates,
    charges,
    leaf_basis,
    transfer,
    skeleton,
    send_plan,
    near_lists,
    near_count,
    far_lists,
):
    points = charges.shape[2]
    rank = leaf_basis.shape[1]
    devices = send_plan.shape[1]
    scales = (
        float(points * (near_lists.shape[1] + 1)) ** (-0.5),
        float(far_lists.shape[1] * rank) ** (-0.5),
    )
    comps = jnp.transpose(coordinates, (1, 0, 2))
    skel = jnp.transpose(skeleton, (1, 0, 2))
    packed = pack(jnp.transpose(send_plan, (0, 2, 1))[0], comps, charges)
    ghosts = lax.all_to_all(packed, AXES, split_axis=0, concat_axis=0, tiled=True)
    payload = parent_payload(charges, leaf_basis, transfer, skel)
    payload = ring_copies(payload, devices // RING)
    targets, items, starts, near = local_near(near_lists.T, near_count, comps, charges)
    apart = (lax.axis_index("x") - (far_lists >> 8)) & 3
    codes = ((far_lists >> 3) & 31) << 8 | (far_lists >> 2 & 1) << 4 | apart << 2 | far_lists & 3
    payload, ghosts, near, codes = lax.optimization_barrier((payload, ghosts, near, codes))
    parents = lax.all_to_all(payload, AXES[1:], split_axis=0, concat_axis=0, tiled=True)
    near = ghost_near(items, starts, ghosts, targets, near)
    return finish(codes, parents, skel, transfer, leaf_basis, near, scales)


def solution(mesh):
    grp, sub = mesh.shape["grp"], mesh.shape["sub"]
    sizes = (grp, RING, RING, sub // (RING * RING))
    apart = Mesh(mesh.devices.reshape(sizes), AXES)
    split3 = P(AXES, None, None)
    in_specs = (split3,) * 6 + (P(AXES, None), P(AXES), P(AXES, None))
    return jax.shard_map(body, mesh=apart, in_specs=in_specs, out_specs=split3, check_vma=False)
```

```python
import functools

import jax
import jax.numpy as jnp
from jax import lax
from jax.experimental import pallas as pl
from jax.experimental.pallas import tpu as pltpu
from jax.sharding import Mesh
from jax.sharding import PartitionSpec as P

SOFTENING = 0.01
AXES = ("x", "y", "z", "core")
RING = 4
BF16 = jnp.bfloat16
F32 = jnp.float32
I32 = jnp.int32
MIB = 1024 * 1024
VMEM_LIMIT = 62 * MIB
GROUP = 8
UNROLL = 32

SMEM = pl.BlockSpec(memory_space=pltpu.SMEM)
VMEM = pl.BlockSpec(memory_space=pltpu.VMEM)
HBM = pl.BlockSpec(memory_space=pltpu.HBM)


def fetch(source, target, semaphore):
    copy = pltpu.make_async_copy(source, target, semaphore)
    copy.start()
    return copy


def whole(shape):
    return pl.BlockSpec(shape, lambda *_: (0,) * len(shape))


def dot_nt(a, b):
    return lax.dot_general(a, b, (((1,), (1,)), ((), ())), preferred_element_type=F32)


def dot_nn(a, b):
    return lax.dot_general(a, b, (((1,), (0,)), ((), ())), preferred_element_type=F32)


def store_rows(table, comps):
    count = comps.shape[1]
    for k in range(8):
        for h in range(2):
            rows = jnp.zeros((count, 128), F32)
            if k % 4 < 3:
                rows = comps[k % 4, :, 128 * h : 128 * h + 128].astype(F32)
            table[h, pl.ds(k, count, stride=8), :] = rows


def pack_kernel(
    plan_hbm, comps_hbm, charges_hbm, out_hbm, comps, charges, table, out, plan, sems
):
    first = fetch(comps_hbm, comps, sems.at[0])
    second = fetch(charges_hbm, charges, sems.at[1])
    third = fetch(plan_hbm, plan, sems.at[2])
    first.wait()
    leaves = comps.shape[1]
    for t in range(3):
        for n in range(8):
            k, h = divmod((2 * t + n) % 6, 2)
            rows = comps[k, :, 128 * h : 128 * h + 128].astype(F32)
            table[t, pl.ds(n, leaves, stride=8), :] = rows
    second.wait()
    third.wait()
    place = lax.broadcasted_iota(I32, (8, 128), 0)

    def one(e):
        rows = [plan[c, e] for c in range(4)]
        for c in range(4):
            for h in range(2):
                lanes = slice(128 * h, 128 * h + 128)
                first_row = 64 * h + 16 * c
                out[e, first_row : first_row + 16, :] = charges[rows[c], :, lanes]
        six = []
        for t, split in ((0, 6), (1, 4), (2, 2)):
            front = table[t, pl.ds(pl.multiple_of(8 * rows[t], 8), 8), :]
            back = table[t, pl.ds(pl.multiple_of(8 * rows[t + 1], 8), 8), :]
            six.append(jnp.where(place < split, front, back))
        out[e, 128:152, :] = jnp.concatenate(six, axis=0).astype(BF16)

    def four(e):
        for n in range(4):
            one(e + n)
        return 0

    pieces = sems.shape[0] - 3
    size = out.shape[0] // pieces

    def piece(q):
        span = pl.ds(q * size, size)
        return pltpu.make_async_copy(out.at[span], out_hbm.at[span], sems.at[3 + q])

    def some(q, _):
        lax.fori_loop(0, size // 4, lambda n, _: four(q * size + 4 * n), 0)
        piece(q).start()
        return 0

    lax.fori_loop(0, pieces, some, 0)
    for q in range(pieces):
        piece(q).wait()


def pack(plan, comps, charges):
    leaves = charges.shape[0]
    devices = plan.shape[1]
    return pl.pallas_call(
        pack_kernel,
        out_shape=jax.ShapeDtypeStruct((devices, 152, 128), BF16),
        in_specs=[HBM, HBM, HBM],
        out_specs=HBM,
        scratch_shapes=[
            pltpu.VMEM(comps.shape, BF16),
            pltpu.VMEM(charges.shape, BF16),
            pltpu.VMEM((3, leaves * 8, 128), F32),
            pltpu.VMEM((devices, 152, 128), BF16),
            pltpu.SMEM(plan.shape, I32),
            pltpu.SemaphoreType.DMA((3 + 8,)),
        ],
        compiler_params=pltpu.CompilerParams(vmem_limit_bytes=VMEM_LIMIT),
        cost_estimate=pl.CostEstimate(flops=0, bytes_accessed=6 * MIB, transcendentals=0),
        name="pack",
    )(plan, comps, charges)


def own_blocks():
    row = lax.broadcasted_iota(I32, (64, 256), 0) // 16
    return row == lax.broadcasted_iota(I32, (64, 256), 1) // 64


def moments_kernel(charges, basis, transfer, skel, out, table):
    own = own_blocks()

    def parent(p):
        total = jnp.zeros((16, 64), F32)
        for quad in range(2):
            leaf = p * GROUP + 4 * quad
            sources = charges[pl.ds(leaf, 4)].reshape(64, 256)
            pairs = dot_nt(sources, basis[pl.ds(leaf, 4)].reshape(256, 256))
            pairs = jnp.where(own, pairs, F32(0.0))
            moment = pairs[0:16] + pairs[16:32] + pairs[32:48] + pairs[48:64]
            total = total + dot_nn(
                moment.astype(BF16), transfer[pl.ds(leaf, 4)].reshape(256, 64)
            )
        return total

    for a in range(4):
        both = jnp.concatenate([parent(a), parent(a + 4)], axis=1).astype(BF16)
        out[16 * a : 16 * a + 16, :] = both
    table[...] = jnp.zeros_like(table)
    for k in range(3):
        rows = skel[k].astype(F32)
        table[pl.ds(k, 4, stride=3), :] = jnp.concatenate([rows[0:4], rows[4:8]], axis=1)
    out[64:80, :] = table[...].astype(BF16)


def parent_payload(charges, basis, transfer, skel):
    return pl.pallas_call(
        moments_kernel,
        out_shape=jax.ShapeDtypeStruct((80, 128), BF16),
        scratch_shapes=[pltpu.VMEM((16, 128), F32)],
        compiler_params=pltpu.CompilerParams(vmem_limit_bytes=VMEM_LIMIT),
        cost_estimate=pl.CostEstimate(flops=10**8, bytes_accessed=4 * MIB, transcendentals=0),
        name="moments",
    )(charges, basis, transfer, skel)


def ring_kernel(*refs):
    pieces, (out, rows, held, sems) = refs[:-4], refs[-4:]
    for t, piece in enumerate(pieces):
        held[64 * t : 64 * t + 64, :] = piece[0:64, :]
        rows[12 * t : 12 * t + 16, :] = piece[64:80, :].astype(F32)
    held[256:304, :] = rows[0:48, :].astype(BF16)
    leaving = [fetch(held, out.at[g], sems.at[g]) for g in range(out.shape[0])]
    for copy in leaving:
        copy.wait()


def ring_copies(payload, groups):
    pieces = [payload]
    for dx in range(1, RING):
        pieces.append(lax.ppermute(payload, "x", [(x, (x + dx) % RING) for x in range(RING)]))
    lanes = payload.shape[1]
    return pl.pallas_call(
        ring_kernel,
        out_shape=jax.ShapeDtypeStruct((groups, 304, lanes), BF16),
        in_specs=[VMEM] * RING,
        out_specs=HBM,
        scratch_shapes=[
            pltpu.VMEM((64, lanes), F32),
            pltpu.VMEM((304, lanes), BF16),
            pltpu.SemaphoreType.DMA((groups,)),
        ],
        compiler_params=pltpu.CompilerParams(vmem_limit_bytes=VMEM_LIMIT),
        cost_estimate=pl.CostEstimate(flops=0, bytes_accessed=3 * MIB, transcendentals=0),
        name="ring_copies",
    )(*pieces)


def near_blocks(items, first, last, targets, row_of, charges_of, acc):
    def some(n, _):
        results = []
        for u in range(UNROLL):
            code = items[n * UNROLL + u]
            target = code >> 10
            source = code & 1023
            place = target & 63
            charge = charges_of(source)
            total = None
            for h in range(2):
                tiles = []
                wide = []
                for k in range(3):
                    row = jnp.broadcast_to(row_of(h, source, k), (16, 128))
                    wide.append(jnp.concatenate([row, row], axis=1).astype(BF16))
                for q in range(8):
                    square = None
                    for k in range(3):
                        off = targets[place, k, 16 * q : 16 * q + 16, :] - wide[k]
                        square = off * off + BF16(SOFTENING) if k == 0 else square + off * off
                    tiles.append(lax.rsqrt(square))
                values = jnp.concatenate(tiles, axis=0)
                values = jnp.concatenate([values[:, :128], values[:, 128:]], axis=0)
                part = dot_nt(charge[h], values)
                total = part if total is None else total + part
            results.append((target, total))
        for target, total in results:
            acc[target] += total
        return 0

    lax.fori_loop(first, last, some, 0)


def local_kernel(
    lists, counts, comps, charges, targets, ghost_items, ghost_start, near, table, acc, items
):
    leaves = charges.shape[0]
    store_rows(table, comps)

    def leaf_entries(leaf, ends):
        local_end, ghost_end = ends
        ghost_start[leaf] = ghost_end
        live_count = counts[leaf]
        items[local_end] = leaf * 1024 + leaf
        local_end = local_end + 1
        for j in range(16):
            slot = lists[j, leaf]
            live = j < live_count
            is_local = slot < 64
            items[local_end] = leaf * 1024 + slot
            ghost_items[ghost_end] = leaf * 1024 + slot - 64
            local_end = local_end + jnp.where(live & is_local, 1, 0)
            ghost_end = ghost_end + jnp.where(live & jnp.logical_not(is_local), 1, 0)
        return local_end, ghost_end

    local_end, ghost_end = lax.fori_loop(0, leaves, leaf_entries, (I32(0), I32(0)))
    for u in range(UNROLL):
        items[local_end + u] = 64 * 1024
        ghost_items[ghost_end + u] = 64 * 1024
    ghost_start[leaves] = ghost_end

    def spread(leaf, _):
        cols = [table[h, pl.ds(pl.multiple_of(8 * leaf, 8), 8), :].T for h in range(2)]
        for k in range(3):
            halves = [jnp.broadcast_to(cols[h][:, k : k + 1], (128, 128)) for h in range(2)]
            targets[leaf, k] = jnp.concatenate(halves, axis=1).astype(BF16)
        return 0

    lax.fori_loop(0, leaves, spread, 0, unroll=2)

    acc[...] = jnp.zeros_like(acc)
    near_blocks(
        items,
        0,
        (local_end + UNROLL - 1) // UNROLL,
        targets,
        lambda h, s, k: table[h, pl.ds(8 * s + k, 1), :],
        lambda s: [charges[s, :, 0:128], charges[s, :, 128:256]],
        acc,
    )
    near[...] = acc[0:leaves]


def local_near(lists, counts, comps, charges):
    leaves, rhs, points = charges.shape
    return pl.pallas_call(
        local_kernel,
        out_shape=(
            jax.ShapeDtypeStruct((leaves, 3, 128, points), BF16),
            jax.ShapeDtypeStruct((leaves * 16 + UNROLL,), I32),
            jax.ShapeDtypeStruct((leaves + 1,), I32),
            jax.ShapeDtypeStruct((leaves, rhs, points), F32),
        ),
        in_specs=[SMEM, SMEM, VMEM, VMEM],
        out_specs=(VMEM, SMEM, SMEM, VMEM),
        scratch_shapes=[
            pltpu.VMEM((2, leaves * 8, 128), F32),
            pltpu.VMEM((leaves + 1, rhs, points), F32),
            pltpu.SMEM((leaves * 17 + UNROLL,), I32),
        ],
        compiler_params=pltpu.CompilerParams(vmem_limit_bytes=VMEM_LIMIT),
        cost_estimate=pl.CostEstimate(
            flops=2 * 10**9, bytes_accessed=15 * MIB, transcendentals=8 * 10**6
        ),
        name="local_near",
    )(lists, counts, comps, charges)


PARTS = 4


def ghost_kernel(
    items_hbm,
    starts_hbm,
    ghosts_hbm,
    targets_hbm,
    start_hbm,
    near_hbm,
    ghosts,
    targets,
    table,
    acc,
    items,
    starts,
    sems,
):
    leaves = start_hbm.shape[0]
    part = leaves // PARTS
    senders = ghosts.shape[0] // PARTS

    def arrival(q):
        span = pl.ds(q * senders, senders)
        return pltpu.make_async_copy(ghosts_hbm.at[span], ghosts.at[span], sems.at[0, q])

    def piece(q):
        span = pl.ds(q * part, part)
        return pltpu.make_async_copy(targets_hbm.at[span], targets.at[span], sems.at[1, q])

    def result(q):
        span = pl.ds(q * part, part)
        return pltpu.make_async_copy(acc.at[span], near_hbm.at[span], sems.at[2, q])

    for q in range(PARTS):
        arrival(q).start()
    begin = fetch(start_hbm, acc.at[pl.ds(0, leaves)], sems.at[3, 0])
    listed = fetch(items_hbm, items, sems.at[3, 1])
    bounds = fetch(starts_hbm, starts, sems.at[3, 2])
    piece(0).start()
    acc[leaves] = jnp.zeros(acc.shape[1:], F32)

    def widen(e, _):
        rows = ghosts[e, 128:152, :].astype(F32)
        table[pl.ds(pl.multiple_of(24 * e, 8), 24), :] = rows
        return 0

    def arrived(q, _):
        arrival(q).wait()
        lax.fori_loop(0, senders, lambda n, _: widen(q * senders + n, _), 0, unroll=8)
        return 0

    lax.fori_loop(0, PARTS, arrived, 0)
    begin.wait()
    listed.wait()
    bounds.wait()
    for q in range(1, PARTS):
        piece(q).start()

    def charges_of(s):
        return [
            ghosts[s >> 2, pl.ds(pl.multiple_of(64 * h + 16 * (s & 3), 16), 16), :]
            for h in range(2)
        ]

    def run(q, _):
        piece(q).wait()
        end = starts[(q + 1) * part]
        last = jnp.where(q == PARTS - 1, (end + UNROLL - 1) // UNROLL, end // UNROLL)
        near_blocks(
            items,
            starts[q * part] // UNROLL,
            last,
            targets,
            lambda h, s, k: table[pl.ds(6 * s + 2 * k + h, 1), :],
            charges_of,
            acc,
        )
        return 0

    lax.fori_loop(0, PARTS, run, 0)
    for q in range(PARTS):
        result(q).start()
    for q in range(PARTS):
        result(q).wait()


def ghost_near(items, starts, ghosts, targets, start):
    leaves, rhs, points = start.shape
    devices = ghosts.shape[0]
    return pl.pallas_call(
        ghost_kernel,
        out_shape=jax.ShapeDtypeStruct(start.shape, F32),
        in_specs=[HBM, HBM, HBM, HBM, HBM],
        out_specs=HBM,
        scratch_shapes=[
            pltpu.VMEM(ghosts.shape, BF16),
            pltpu.VMEM(targets.shape, BF16),
            pltpu.VMEM((devices * 24, 128), F32),
            pltpu.VMEM((leaves + 1, rhs, points), F32),
            pltpu.SMEM(items.shape, I32),
            pltpu.SMEM(starts.shape, I32),
            pltpu.SemaphoreType.DMA((4, PARTS)),
        ],
        compiler_params=pltpu.CompilerParams(vmem_limit_bytes=VMEM_LIMIT),
        cost_estimate=pl.CostEstimate(
            flops=10**10, bytes_accessed=20 * MIB, transcendentals=4 * 10**7
        ),
        name="ghost_near",
    )(items, starts, ghosts, targets, start)


def finish_kernel(
    far,
    parents,
    skel,
    transfer_hbm,
    basis_hbm,
    near_hbm,
    out_hbm,
    out,
    transfer,
    basis,
    near,
    table,
    own,
    local,
    sems,
    *,
    scales,
):
    near_scale, far_scale = scales
    clusters, length = far.shape
    fetches = [
        fetch(source, target, sems.at[n])
        for n, (source, target) in enumerate(
            [
                (transfer_hbm, transfer),
                (basis_hbm, basis),
                (near_hbm, near),
            ]
        )
    ]

    def widen(e, _):
        table[pl.ds(pl.multiple_of(48 * e, 16), 48), :] = parents[e, 256:304, :].astype(F32)
        return 0

    lax.fori_loop(0, parents.shape[0], widen, 0, unroll=4)
    own[...] = jnp.zeros_like(own)
    for k in range(3):
        rows = skel[k].astype(F32)
        own[pl.ds(k, clusters, stride=8), :] = jnp.concatenate([rows, rows], axis=1)

    half = (lax.broadcasted_iota(I32, (16, 128), 1) >= 64).astype(I32)

    def coefficients(p, _):
        cols = own[pl.ds(pl.multiple_of(8 * p, 8), 8), :].T
        target = [
            jnp.broadcast_to(cols[0:64, k : k + 1], (64, 128)).astype(BF16) for k in range(3)
        ]
        target = [jnp.concatenate([t, t], axis=1) for t in target]
        total = jnp.zeros((16, 64), F32)
        for first in range(0, length, 2):
            moments = []
            rows = [[], [], []]
            for f in (first, first + 1):
                code = far[p, min(f, length - 1)]
                group, inner, wanted = code >> 8, code & 15, (code >> 4) & 1
                wanted = wanted if f < length else 2
                moment = parents[group, pl.ds(pl.multiple_of(16 * inner, 16), 16), :]
                moments.append(jnp.where(half == wanted, moment.astype(F32), F32(0.0)))
                for k in range(3):
                    row = table[pl.ds(48 * group + 3 * inner + k, 1), :]
                    rows[k].append(jnp.broadcast_to(row, (16, 128)))
            rows = [jnp.concatenate(r, axis=1).astype(BF16) for r in rows]
            tiles = []
            for q in range(4):
                square = None
                for k in range(3):
                    off = target[k][16 * q : 16 * q + 16, :] - rows[k]
                    square = off * off + BF16(SOFTENING) if k == 0 else square + off * off
                tiles.append(lax.rsqrt(square))
            moment = jnp.concatenate(moments, axis=1).astype(BF16)
            total = total + dot_nt(moment, jnp.concatenate(tiles, axis=0))
        local[p] = (far_scale * total).astype(BF16)
        return 0

    lax.fori_loop(0, clusters, coefficients, 0, unroll=2)

    for copy in fetches:
        copy.wait()
    block = own_blocks()

    def leaves_of(p):
        coef = local[p]
        coef = jnp.concatenate([coef, coef, coef, coef], axis=0)
        for quad in range(2):
            leaf = p * GROUP + 4 * quad
            child = dot_nt(coef, transfer[pl.ds(leaf, 4)].reshape(256, 64))
            child = jnp.where(block, child, F32(0.0)).astype(BF16)
            field = dot_nn(child, basis[pl.ds(leaf, 4)].reshape(256, 256))
            total = near_scale * near[pl.ds(leaf, 4)] + field.reshape(4, 16, 256)
            out[pl.ds(leaf, 4)] = total.astype(BF16)

    def half_of(n):
        span = pl.ds(n * 4 * GROUP, 4 * GROUP)
        return pltpu.make_async_copy(out.at[span], out_hbm.at[span], sems.at[3 + n])

    def half_leaves(n, _):
        for p in range(4):
            leaves_of(4 * n + p)
        half_of(n).start()
        return 0

    lax.fori_loop(0, 2, half_leaves, 0)
    for n in range(2):
        half_of(n).wait()


def finish(far, parents, skel, transfer, basis, near, scales):
    devices = parents.shape[0] * RING
    return pl.pallas_call(
        functools.partial(finish_kernel, scales=scales),
        out_shape=jax.ShapeDtypeStruct(near.shape, BF16),
        in_specs=[SMEM, VMEM, VMEM, HBM, HBM, HBM],
        out_specs=HBM,
        scratch_shapes=[
            pltpu.VMEM(near.shape, BF16),
            pltpu.VMEM(transfer.shape, BF16),
            pltpu.VMEM(basis.shape, BF16),
            pltpu.VMEM(near.shape, F32),
            pltpu.VMEM((devices * 12, 128), F32),
            pltpu.VMEM((64, 128), F32),
            pltpu.VMEM((far.shape[0], 16, 64), BF16),
            pltpu.SemaphoreType.DMA((3 + 2,)),
        ],
        compiler_params=pltpu.CompilerParams(vmem_limit_bytes=VMEM_LIMIT),
        cost_estimate=pl.CostEstimate(
            flops=10**8, bytes_accessed=8 * MIB, transcendentals=10**6
        ),
        name="finish",
    )(far, parents, skel, transfer, basis, near)


def body(
    coordinates,
    charges,
    leaf_basis,
    transfer,
    skeleton,
    send_plan,
    near_lists,
    near_count,
    far_lists,
):
    points = charges.shape[2]
    rank = leaf_basis.shape[1]
    devices = send_plan.shape[1]
    scales = (
        float(points * (near_lists.shape[1] + 1)) ** (-0.5),
        float(far_lists.shape[1] * rank) ** (-0.5),
    )
    comps = jnp.transpose(coordinates, (1, 0, 2))
    skel = jnp.transpose(skeleton, (1, 0, 2))
    packed = pack(jnp.transpose(send_plan, (0, 2, 1))[0], comps, charges)
    ghosts = lax.all_to_all(packed, AXES, split_axis=0, concat_axis=0, tiled=True)
    payload = parent_payload(charges, leaf_basis, transfer, skel)
    payload = ring_copies(payload, devices // RING)
    targets, items, starts, near = local_near(near_lists.T, near_count, comps, charges)
    apart = (lax.axis_index("x") - (far_lists >> 8)) & 3
    codes = ((far_lists >> 3) & 31) << 8 | (far_lists >> 2 & 1) << 4 | apart << 2 | far_lists & 3
    payload, ghosts, near, codes = lax.optimization_barrier((payload, ghosts, near, codes))
    parents = lax.all_to_all(payload, AXES[1:], split_axis=0, concat_axis=0, tiled=True)
    near = ghost_near(items, starts, ghosts, targets, near)
    return finish(codes, parents, skel, transfer, leaf_basis, near, scales)


def solution(mesh):
    grp, sub = mesh.shape["grp"], mesh.shape["sub"]
    sizes = (grp, RING, RING, sub // (RING * RING))
    apart = Mesh(mesh.devices.reshape(sizes), AXES)
    split3 = P(AXES, None, None)
    in_specs = (split3,) * 6 + (P(AXES, None), P(AXES), P(AXES, None))
    return jax.shard_map(body, mesh=apart, in_specs=in_specs, out_specs=split3, check_vma=False)
```

```python
import functools

import jax
import jax.numpy as jnp
from jax import lax
from jax.experimental import pallas as pl
from jax.experimental.pallas import tpu as pltpu
from jax.sharding import Mesh
from jax.sharding import PartitionSpec as P

SOFTENING = 0.01
AXES = ("x", "y", "z", "core")
RING = 4
BF16 = jnp.bfloat16
F32 = jnp.float32
I32 = jnp.int32
MIB = 1024 * 1024
VMEM_LIMIT = 62 * MIB
GROUP = 8
UNROLL = 32

SMEM = pl.BlockSpec(memory_space=pltpu.SMEM)
VMEM = pl.BlockSpec(memory_space=pltpu.VMEM)
HBM = pl.BlockSpec(memory_space=pltpu.HBM)


def fetch(source, target, semaphore):
    copy = pltpu.make_async_copy(source, target, semaphore)
    copy.start()
    return copy


def whole(shape):
    return pl.BlockSpec(shape, lambda *_: (0,) * len(shape))


def dot_nt(a, b):
    return lax.dot_general(a, b, (((1,), (1,)), ((), ())), preferred_element_type=F32)


def dot_nn(a, b):
    return lax.dot_general(a, b, (((1,), (0,)), ((), ())), preferred_element_type=F32)


def store_rows(table, comps):
    count = comps.shape[1]
    for k in range(8):
        for h in range(2):
            rows = jnp.zeros((count, 128), F32)
            if k % 4 < 3:
                rows = comps[k % 4, :, 128 * h : 128 * h + 128].astype(F32)
            table[h, pl.ds(k, count, stride=8), :] = rows


def pack_kernel(
    plan_hbm, comps_hbm, charges_hbm, out_hbm, comps, charges, table, out, plan, sems
):
    first = fetch(comps_hbm, comps, sems.at[0])
    second = fetch(charges_hbm, charges, sems.at[1])
    third = fetch(plan_hbm, plan, sems.at[2])
    first.wait()
    leaves = comps.shape[1]
    for t in range(3):
        for n in range(8):
            k, h = divmod((2 * t + n) % 6, 2)
            rows = comps[k, :, 128 * h : 128 * h + 128].astype(F32)
            table[t, pl.ds(n, leaves, stride=8), :] = rows
    second.wait()
    third.wait()
    place = lax.broadcasted_iota(I32, (8, 128), 0)

    def one(e):
        rows = [plan[c, e] for c in range(4)]
        for c in range(4):
            for h in range(2):
                lanes = slice(128 * h, 128 * h + 128)
                first_row = 64 * h + 16 * c
                out[e, first_row : first_row + 16, :] = charges[rows[c], :, lanes]
        six = []
        for t, split in ((0, 6), (1, 4), (2, 2)):
            front = table[t, pl.ds(pl.multiple_of(8 * rows[t], 8), 8), :]
            back = table[t, pl.ds(pl.multiple_of(8 * rows[t + 1], 8), 8), :]
            six.append(jnp.where(place < split, front, back))
        out[e, 128:152, :] = jnp.concatenate(six, axis=0).astype(BF16)

    def four(e):
        for n in range(4):
            one(e + n)
        return 0

    pieces = sems.shape[0] - 3
    size = out.shape[0] // pieces

    def piece(q):
        span = pl.ds(q * size, size)
        return pltpu.make_async_copy(out.at[span], out_hbm.at[span], sems.at[3 + q])

    def some(q, _):
        lax.fori_loop(0, size // 4, lambda n, _: four(q * size + 4 * n), 0)
        piece(q).start()
        return 0

    lax.fori_loop(0, pieces, some, 0)
    for q in range(pieces):
        piece(q).wait()


def pack(plan, comps, charges):
    leaves = charges.shape[0]
    devices = plan.shape[1]
    return pl.pallas_call(
        pack_kernel,
        out_shape=jax.ShapeDtypeStruct((devices, 152, 128), BF16),
        in_specs=[HBM, HBM, HBM],
        out_specs=HBM,
        scratch_shapes=[
            pltpu.VMEM(comps.shape, BF16),
            pltpu.VMEM(charges.shape, BF16),
            pltpu.VMEM((3, leaves * 8, 128), F32),
            pltpu.VMEM((devices, 152, 128), BF16),
            pltpu.SMEM(plan.shape, I32),
            pltpu.SemaphoreType.DMA((3 + 8,)),
        ],
        compiler_params=pltpu.CompilerParams(vmem_limit_bytes=VMEM_LIMIT),
        cost_estimate=pl.CostEstimate(flops=0, bytes_accessed=6 * MIB, transcendentals=0),
        name="pack",
    )(plan, comps, charges)


def own_blocks():
    row = lax.broadcasted_iota(I32, (64, 256), 0) // 16
    return row == lax.broadcasted_iota(I32, (64, 256), 1) // 64


def moments_kernel(charges, basis, transfer, skel, out, table):
    own = own_blocks()

    def parent(p):
        total = jnp.zeros((16, 64), F32)
        for quad in range(2):
            leaf = p * GROUP + 4 * quad
            sources = charges[pl.ds(leaf, 4)].reshape(64, 256)
            pairs = dot_nt(sources, basis[pl.ds(leaf, 4)].reshape(256, 256))
            pairs = jnp.where(own, pairs, F32(0.0))
            moment = pairs[0:16] + pairs[16:32] + pairs[32:48] + pairs[48:64]
            total = total + dot_nn(
                moment.astype(BF16), transfer[pl.ds(leaf, 4)].reshape(256, 64)
            )
        return total

    for a in range(4):
        both = jnp.concatenate([parent(a), parent(a + 4)], axis=1).astype(BF16)
        out[16 * a : 16 * a + 16, :] = both
    table[...] = jnp.zeros_like(table)
    for k in range(3):
        rows = skel[k].astype(F32)
        table[pl.ds(k, 4, stride=3), :] = jnp.concatenate([rows[0:4], rows[4:8]], axis=1)
    out[64:80, :] = table[...].astype(BF16)


def parent_payload(charges, basis, transfer, skel):
    return pl.pallas_call(
        moments_kernel,
        out_shape=jax.ShapeDtypeStruct((80, 128), BF16),
        scratch_shapes=[pltpu.VMEM((16, 128), F32)],
        compiler_params=pltpu.CompilerParams(vmem_limit_bytes=VMEM_LIMIT),
        cost_estimate=pl.CostEstimate(flops=10**8, bytes_accessed=4 * MIB, transcendentals=0),
        name="moments",
    )(charges, basis, transfer, skel)


def ring_kernel(*refs):
    pieces, (out, rows, held, sems) = refs[:-4], refs[-4:]
    for t, piece in enumerate(pieces):
        held[64 * t : 64 * t + 64, :] = piece[0:64, :]
        rows[12 * t : 12 * t + 16, :] = piece[64:80, :].astype(F32)
    held[256:304, :] = rows[0:48, :].astype(BF16)
    leaving = [fetch(held, out.at[g], sems.at[g]) for g in range(out.shape[0])]
    for copy in leaving:
        copy.wait()


def ring_copies(payload, groups):
    pieces = [payload]
    for dx in range(1, RING):
        pieces.append(lax.ppermute(payload, "x", [(x, (x + dx) % RING) for x in range(RING)]))
    lanes = payload.shape[1]
    return pl.pallas_call(
        ring_kernel,
        out_shape=jax.ShapeDtypeStruct((groups, 304, lanes), BF16),
        in_specs=[VMEM] * RING,
        out_specs=HBM,
        scratch_shapes=[
            pltpu.VMEM((64, lanes), F32),
            pltpu.VMEM((304, lanes), BF16),
            pltpu.SemaphoreType.DMA((groups,)),
        ],
        compiler_params=pltpu.CompilerParams(vmem_limit_bytes=16 * MIB),
        cost_estimate=pl.CostEstimate(flops=0, bytes_accessed=3 * MIB, transcendentals=0),
        name="ring_copies",
    )(*pieces)


def near_blocks(items, first, last, targets, row_of, charges_of, acc):
    def some(n, _):
        results = []
        for u in range(UNROLL):
            code = items[n * UNROLL + u]
            target = code >> 10
            source = code & 1023
            place = target & 63
            charge = charges_of(source)
            total = None
            for h in range(2):
                tiles = []
                wide = []
                for k in range(3):
                    row = jnp.broadcast_to(row_of(h, source, k), (16, 128))
                    wide.append(jnp.concatenate([row, row], axis=1).astype(BF16))
                for q in range(8):
                    square = None
                    for k in range(3):
                        off = targets[place, k, 16 * q : 16 * q + 16, :] - wide[k]
                        square = off * off + BF16(SOFTENING) if k == 0 else square + off * off
                    tiles.append(lax.rsqrt(square))
                values = jnp.concatenate(tiles, axis=0)
                values = jnp.concatenate([values[:, :128], values[:, 128:]], axis=0)
                part = dot_nt(charge[h], values)
                total = part if total is None else total + part
            results.append((target, total))
        for target, total in results:
            acc[target] += total
        return 0

    lax.fori_loop(first, last, some, 0)


def local_kernel(
    lists, counts, comps, charges, targets, ghost_items, ghost_start, near, table, acc, items
):
    leaves = charges.shape[0]
    store_rows(table, comps)

    def leaf_entries(leaf, ends):
        local_end, ghost_end = ends
        ghost_start[leaf] = ghost_end
        live_count = counts[leaf]
        items[local_end] = leaf * 1024 + leaf
        local_end = local_end + 1
        for j in range(16):
            slot = lists[j, leaf]
            live = j < live_count
            is_local = slot < 64
            items[local_end] = leaf * 1024 + slot
            ghost_items[ghost_end] = leaf * 1024 + slot - 64
            local_end = local_end + jnp.where(live & is_local, 1, 0)
            ghost_end = ghost_end + jnp.where(live & jnp.logical_not(is_local), 1, 0)
        return local_end, ghost_end

    local_end, ghost_end = lax.fori_loop(0, leaves, leaf_entries, (I32(0), I32(0)))
    for u in range(UNROLL):
        items[local_end + u] = 64 * 1024
        ghost_items[ghost_end + u] = 64 * 1024
    ghost_start[leaves] = ghost_end

    def spread(leaf, _):
        cols = [table[h, pl.ds(pl.multiple_of(8 * leaf, 8), 8), :].T for h in range(2)]
        for k in range(3):
            halves = [jnp.broadcast_to(cols[h][:, k : k + 1], (128, 128)) for h in range(2)]
            targets[leaf, k] = jnp.concatenate(halves, axis=1).astype(BF16)
        return 0

    lax.fori_loop(0, leaves, spread, 0, unroll=2)

    acc[...] = jnp.zeros_like(acc)
    near_blocks(
        items,
        0,
        (local_end + UNROLL - 1) // UNROLL,
        targets,
        lambda h, s, k: table[h, pl.ds(8 * s + k, 1), :],
        lambda s: [charges[s, :, 0:128], charges[s, :, 128:256]],
        acc,
    )
    near[...] = acc[0:leaves]


def local_near(lists, counts, comps, charges):
    leaves, rhs, points = charges.shape
    return pl.pallas_call(
        local_kernel,
        out_shape=(
            jax.ShapeDtypeStruct((leaves, 3, 128, points), BF16),
            jax.ShapeDtypeStruct((leaves * 16 + UNROLL,), I32),
            jax.ShapeDtypeStruct((leaves + 1,), I32),
            jax.ShapeDtypeStruct((leaves, rhs, points), F32),
        ),
        in_specs=[SMEM, SMEM, VMEM, VMEM],
        out_specs=(VMEM, SMEM, SMEM, VMEM),
        scratch_shapes=[
            pltpu.VMEM((2, leaves * 8, 128), F32),
            pltpu.VMEM((leaves + 1, rhs, points), F32),
            pltpu.SMEM((leaves * 17 + UNROLL,), I32),
        ],
        compiler_params=pltpu.CompilerParams(vmem_limit_bytes=VMEM_LIMIT),
        cost_estimate=pl.CostEstimate(
            flops=2 * 10**9, bytes_accessed=15 * MIB, transcendentals=8 * 10**6
        ),
        name="local_near",
    )(lists, counts, comps, charges)


PARTS = 4


def ghost_kernel(
    items_hbm,
    starts_hbm,
    ghosts_hbm,
    targets_hbm,
    start_hbm,
    near_hbm,
    ghosts,
    targets,
    table,
    acc,
    items,
    starts,
    sems,
):
    leaves = start_hbm.shape[0]
    part = leaves // PARTS
    senders = ghosts.shape[0] // PARTS

    def arrival(q):
        span = pl.ds(q * senders, senders)
        return pltpu.make_async_copy(ghosts_hbm.at[span], ghosts.at[span], sems.at[0, q])

    def piece(q):
        span = pl.ds(q * part, part)
        return pltpu.make_async_copy(targets_hbm.at[span], targets.at[span], sems.at[1, q])

    def result(q):
        span = pl.ds(q * part, part)
        return pltpu.make_async_copy(acc.at[span], near_hbm.at[span], sems.at[2, q])

    for q in range(PARTS):
        arrival(q).start()
    begin = fetch(start_hbm, acc.at[pl.ds(0, leaves)], sems.at[3, 0])
    listed = fetch(items_hbm, items, sems.at[3, 1])
    bounds = fetch(starts_hbm, starts, sems.at[3, 2])
    piece(0).start()
    acc[leaves] = jnp.zeros(acc.shape[1:], F32)

    def widen(e, _):
        rows = ghosts[e, 128:152, :].astype(F32)
        table[pl.ds(pl.multiple_of(24 * e, 8), 24), :] = rows
        return 0

    def arrived(q, _):
        arrival(q).wait()
        lax.fori_loop(0, senders, lambda n, _: widen(q * senders + n, _), 0, unroll=8)
        return 0

    lax.fori_loop(0, PARTS, arrived, 0)
    begin.wait()
    listed.wait()
    bounds.wait()
    for q in range(1, PARTS):
        piece(q).start()

    def charges_of(s):
        return [
            ghosts[s >> 2, pl.ds(pl.multiple_of(64 * h + 16 * (s & 3), 16), 16), :]
            for h in range(2)
        ]

    def run(q, _):
        piece(q).wait()
        end = starts[(q + 1) * part]
        last = jnp.where(q == PARTS - 1, (end + UNROLL - 1) // UNROLL, end // UNROLL)
        near_blocks(
            items,
            starts[q * part] // UNROLL,
            last,
            targets,
            lambda h, s, k: table[pl.ds(6 * s + 2 * k + h, 1), :],
            charges_of,
            acc,
        )
        return 0

    lax.fori_loop(0, PARTS, run, 0)
    for q in range(PARTS):
        result(q).start()
    for q in range(PARTS):
        result(q).wait()


def ghost_near(items, starts, ghosts, targets, start):
    leaves, rhs, points = start.shape
    devices = ghosts.shape[0]
    return pl.pallas_call(
        ghost_kernel,
        out_shape=jax.ShapeDtypeStruct(start.shape, F32),
        in_specs=[HBM, HBM, HBM, HBM, HBM],
        out_specs=HBM,
        scratch_shapes=[
            pltpu.VMEM(ghosts.shape, BF16),
            pltpu.VMEM(targets.shape, BF16),
            pltpu.VMEM((devices * 24, 128), F32),
            pltpu.VMEM((leaves + 1, rhs, points), F32),
            pltpu.SMEM(items.shape, I32),
            pltpu.SMEM(starts.shape, I32),
            pltpu.SemaphoreType.DMA((4, PARTS)),
        ],
        compiler_params=pltpu.CompilerParams(vmem_limit_bytes=VMEM_LIMIT),
        cost_estimate=pl.CostEstimate(
            flops=10**10, bytes_accessed=20 * MIB, transcendentals=4 * 10**7
        ),
        name="ghost_near",
    )(items, starts, ghosts, targets, start)


def finish_kernel(
    far,
    parents,
    skel,
    transfer_hbm,
    basis_hbm,
    near_hbm,
    out_hbm,
    out,
    transfer,
    basis,
    near,
    table,
    own,
    local,
    sems,
    *,
    scales,
):
    near_scale, far_scale = scales
    clusters, length = far.shape
    fetches = [
        fetch(source, target, sems.at[n])
        for n, (source, target) in enumerate(
            [
                (transfer_hbm, transfer),
                (basis_hbm, basis),
                (near_hbm, near),
            ]
        )
    ]

    def widen(e, _):
        table[pl.ds(pl.multiple_of(48 * e, 16), 48), :] = parents[e, 256:304, :].astype(F32)
        return 0

    lax.fori_loop(0, parents.shape[0], widen, 0, unroll=4)
    own[...] = jnp.zeros_like(own)
    for k in range(3):
        rows = skel[k].astype(F32)
        own[pl.ds(k, clusters, stride=8), :] = jnp.concatenate([rows, rows], axis=1)

    half = (lax.broadcasted_iota(I32, (16, 128), 1) >= 64).astype(I32)

    def coefficients(p, _):
        cols = own[pl.ds(pl.multiple_of(8 * p, 8), 8), :].T
        target = [
            jnp.broadcast_to(cols[0:64, k : k + 1], (64, 128)).astype(BF16) for k in range(3)
        ]
        target = [jnp.concatenate([t, t], axis=1) for t in target]
        total = jnp.zeros((16, 64), F32)
        for first in range(0, length, 2):
            moments = []
            rows = [[], [], []]
            for f in (first, first + 1):
                code = far[p, min(f, length - 1)]
                group, inner, wanted = code >> 8, code & 15, (code >> 4) & 1
                wanted = wanted if f < length else 2
                moment = parents[group, pl.ds(pl.multiple_of(16 * inner, 16), 16), :]
                moments.append(jnp.where(half == wanted, moment.astype(F32), F32(0.0)))
                for k in range(3):
                    row = table[pl.ds(48 * group + 3 * inner + k, 1), :]
                    rows[k].append(jnp.broadcast_to(row, (16, 128)))
            rows = [jnp.concatenate(r, axis=1).astype(BF16) for r in rows]
            tiles = []
            for q in range(4):
                square = None
                for k in range(3):
                    off = target[k][16 * q : 16 * q + 16, :] - rows[k]
                    square = off * off + BF16(SOFTENING) if k == 0 else square + off * off
                tiles.append(lax.rsqrt(square))
            moment = jnp.concatenate(moments, axis=1).astype(BF16)
            total = total + dot_nt(moment, jnp.concatenate(tiles, axis=0))
        local[p] = (far_scale * total).astype(BF16)
        return 0

    lax.fori_loop(0, clusters, coefficients, 0, unroll=2)

    for copy in fetches:
        copy.wait()
    block = own_blocks()

    def leaves_of(p):
        coef = local[p]
        coef = jnp.concatenate([coef, coef, coef, coef], axis=0)
        for quad in range(2):
            leaf = p * GROUP + 4 * quad
            child = dot_nt(coef, transfer[pl.ds(leaf, 4)].reshape(256, 64))
            child = jnp.where(block, child, F32(0.0)).astype(BF16)
            field = dot_nn(child, basis[pl.ds(leaf, 4)].reshape(256, 256))
            total = near_scale * near[pl.ds(leaf, 4)] + field.reshape(4, 16, 256)
            out[pl.ds(leaf, 4)] = total.astype(BF16)

    def half_of(n):
        span = pl.ds(n * 4 * GROUP, 4 * GROUP)
        return pltpu.make_async_copy(out.at[span], out_hbm.at[span], sems.at[3 + n])

    def half_leaves(n, _):
        for p in range(4):
            leaves_of(4 * n + p)
        half_of(n).start()
        return 0

    lax.fori_loop(0, 2, half_leaves, 0)
    for n in range(2):
        half_of(n).wait()


def finish(far, parents, skel, transfer, basis, near, scales):
    devices = parents.shape[0] * RING
    return pl.pallas_call(
        functools.partial(finish_kernel, scales=scales),
        out_shape=jax.ShapeDtypeStruct(near.shape, BF16),
        in_specs=[SMEM, VMEM, VMEM, HBM, HBM, HBM],
        out_specs=HBM,
        scratch_shapes=[
            pltpu.VMEM(near.shape, BF16),
            pltpu.VMEM(transfer.shape, BF16),
            pltpu.VMEM(basis.shape, BF16),
            pltpu.VMEM(near.shape, F32),
            pltpu.VMEM((devices * 12, 128), F32),
            pltpu.VMEM((64, 128), F32),
            pltpu.VMEM((far.shape[0], 16, 64), BF16),
            pltpu.SemaphoreType.DMA((3 + 2,)),
        ],
        compiler_params=pltpu.CompilerParams(vmem_limit_bytes=VMEM_LIMIT),
        cost_estimate=pl.CostEstimate(
            flops=10**8, bytes_accessed=8 * MIB, transcendentals=10**6
        ),
        name="finish",
    )(far, parents, skel, transfer, basis, near)


def body(
    coordinates,
    charges,
    leaf_basis,
    transfer,
    skeleton,
    send_plan,
    near_lists,
    near_count,
    far_lists,
):
    points = charges.shape[2]
    rank = leaf_basis.shape[1]
    devices = send_plan.shape[1]
    scales = (
        float(points * (near_lists.shape[1] + 1)) ** (-0.5),
        float(far_lists.shape[1] * rank) ** (-0.5),
    )
    comps = jnp.transpose(coordinates, (1, 0, 2))
    skel = jnp.transpose(skeleton, (1, 0, 2))
    packed = pack(jnp.transpose(send_plan, (0, 2, 1))[0], comps, charges)
    ghosts = lax.all_to_all(packed, AXES, split_axis=0, concat_axis=0, tiled=True)
    payload = parent_payload(charges, leaf_basis, transfer, skel)
    payload = ring_copies(payload, devices // RING)
    targets, items, starts, near = local_near(near_lists.T, near_count, comps, charges)
    apart = (lax.axis_index("x") - (far_lists >> 8)) & 3
    codes = ((far_lists >> 3) & 31) << 8 | (far_lists >> 2 & 1) << 4 | apart << 2 | far_lists & 3
    payload, ghosts, near, codes = lax.optimization_barrier((payload, ghosts, near, codes))
    parents = lax.all_to_all(payload, AXES[1:], split_axis=0, concat_axis=0, tiled=True)
    near = ghost_near(items, starts, ghosts, targets, near)
    return finish(codes, parents, skel, transfer, leaf_basis, near, scales)


def solution(mesh):
    grp, sub = mesh.shape["grp"], mesh.shape["sub"]
    sizes = (grp, RING, RING, sub // (RING * RING))
    apart = Mesh(mesh.devices.reshape(sizes), AXES)
    split3 = P(AXES, None, None)
    in_specs = (split3,) * 6 + (P(AXES, None), P(AXES), P(AXES, None))
    return jax.shard_map(body, mesh=apart, in_specs=in_specs, out_specs=split3, check_vma=False)
```

```python
import functools

import jax
import jax.numpy as jnp
from jax import lax
from jax.experimental import pallas as pl
from jax.experimental.pallas import tpu as pltpu
from jax.sharding import Mesh
from jax.sharding import PartitionSpec as P

SOFTENING = 0.01
AXES = ("x", "y", "z", "core")
RING = 4
BF16 = jnp.bfloat16
F32 = jnp.float32
I32 = jnp.int32
MIB = 1024 * 1024
VMEM_LIMIT = 62 * MIB
GROUP = 8
UNROLL = 32

SMEM = pl.BlockSpec(memory_space=pltpu.SMEM)
VMEM = pl.BlockSpec(memory_space=pltpu.VMEM)
HBM = pl.BlockSpec(memory_space=pltpu.HBM)


def fetch(source, target, semaphore):
    copy = pltpu.make_async_copy(source, target, semaphore)
    copy.start()
    return copy


def whole(shape):
    return pl.BlockSpec(shape, lambda *_: (0,) * len(shape))


def dot_nt(a, b):
    return lax.dot_general(a, b, (((1,), (1,)), ((), ())), preferred_element_type=F32)


def dot_nn(a, b):
    return lax.dot_general(a, b, (((1,), (0,)), ((), ())), preferred_element_type=F32)


def store_rows(table, comps):
    count = comps.shape[1]
    for k in range(8):
        for h in range(2):
            rows = jnp.zeros((count, 128), F32)
            if k % 4 < 3:
                rows = comps[k % 4, :, 128 * h : 128 * h + 128].astype(F32)
            table[h, pl.ds(k, count, stride=8), :] = rows


def pack_kernel(
    plan_hbm, comps_hbm, charges_hbm, out_hbm, comps, charges, table, out, plan, sems
):
    first = fetch(comps_hbm, comps, sems.at[0])
    second = fetch(charges_hbm, charges, sems.at[1])
    third = fetch(plan_hbm, plan, sems.at[2])
    first.wait()
    leaves = comps.shape[1]
    for t in range(3):
        for n in range(8):
            k, h = divmod((2 * t + n) % 6, 2)
            rows = comps[k, :, 128 * h : 128 * h + 128].astype(F32)
            table[t, pl.ds(n, leaves, stride=8), :] = rows
    second.wait()
    third.wait()
    place = lax.broadcasted_iota(I32, (8, 128), 0)

    def one(e):
        rows = [plan[c, e] for c in range(4)]
        for c in range(4):
            for h in range(2):
                lanes = slice(128 * h, 128 * h + 128)
                first_row = 64 * h + 16 * c
                out[e, first_row : first_row + 16, :] = charges[rows[c], :, lanes]
        six = []
        for t, split in ((0, 6), (1, 4), (2, 2)):
            front = table[t, pl.ds(pl.multiple_of(8 * rows[t], 8), 8), :]
            back = table[t, pl.ds(pl.multiple_of(8 * rows[t + 1], 8), 8), :]
            six.append(jnp.where(place < split, front, back))
        out[e, 128:152, :] = jnp.concatenate(six, axis=0).astype(BF16)

    def four(e):
        for n in range(8):
            one(e + n)
        return 0

    pieces = sems.shape[0] - 3
    size = out.shape[0] // pieces

    def piece(q):
        span = pl.ds(q * size, size)
        return pltpu.make_async_copy(out.at[span], out_hbm.at[span], sems.at[3 + q])

    def some(q, _):
        lax.fori_loop(0, size // 8, lambda n, _: four(q * size + 8 * n), 0)
        piece(q).start()
        return 0

    lax.fori_loop(0, pieces, some, 0)
    for q in range(pieces):
        piece(q).wait()


def pack(plan, comps, charges):
    leaves = charges.shape[0]
    devices = plan.shape[1]
    return pl.pallas_call(
        pack_kernel,
        out_shape=jax.ShapeDtypeStruct((devices, 152, 128), BF16),
        in_specs=[HBM, HBM, HBM],
        out_specs=HBM,
        scratch_shapes=[
            pltpu.VMEM(comps.shape, BF16),
            pltpu.VMEM(charges.shape, BF16),
            pltpu.VMEM((3, leaves * 8, 128), F32),
            pltpu.VMEM((devices, 152, 128), BF16),
            pltpu.SMEM(plan.shape, I32),
            pltpu.SemaphoreType.DMA((3 + 8,)),
        ],
        compiler_params=pltpu.CompilerParams(vmem_limit_bytes=VMEM_LIMIT),
        cost_estimate=pl.CostEstimate(flops=0, bytes_accessed=6 * MIB, transcendentals=0),
        name="pack",
    )(plan, comps, charges)


def own_blocks():
    row = lax.broadcasted_iota(I32, (64, 256), 0) // 16
    return row == lax.broadcasted_iota(I32, (64, 256), 1) // 64


def moments_kernel(charges, basis, transfer, skel, out, table):
    own = own_blocks()

    def parent(p):
        total = jnp.zeros((16, 64), F32)
        for quad in range(2):
            leaf = p * GROUP + 4 * quad
            sources = charges[pl.ds(leaf, 4)].reshape(64, 256)
            pairs = dot_nt(sources, basis[pl.ds(leaf, 4)].reshape(256, 256))
            pairs = jnp.where(own, pairs, F32(0.0))
            moment = pairs[0:16] + pairs[16:32] + pairs[32:48] + pairs[48:64]
            total = total + dot_nn(
                moment.astype(BF16), transfer[pl.ds(leaf, 4)].reshape(256, 64)
            )
        return total

    for a in range(4):
        both = jnp.concatenate([parent(a), parent(a + 4)], axis=1).astype(BF16)
        out[16 * a : 16 * a + 16, :] = both
    table[...] = jnp.zeros_like(table)
    for k in range(3):
        rows = skel[k].astype(F32)
        table[pl.ds(k, 4, stride=3), :] = jnp.concatenate([rows[0:4], rows[4:8]], axis=1)
    out[64:80, :] = table[...].astype(BF16)


def parent_payload(charges, basis, transfer, skel):
    return pl.pallas_call(
        moments_kernel,
        out_shape=jax.ShapeDtypeStruct((80, 128), BF16),
        scratch_shapes=[pltpu.VMEM((16, 128), F32)],
        compiler_params=pltpu.CompilerParams(vmem_limit_bytes=VMEM_LIMIT),
        cost_estimate=pl.CostEstimate(flops=10**8, bytes_accessed=4 * MIB, transcendentals=0),
        name="moments",
    )(charges, basis, transfer, skel)


def ring_kernel(*refs):
    pieces, (out, rows, held, sems) = refs[:-4], refs[-4:]
    for t, piece in enumerate(pieces):
        held[64 * t : 64 * t + 64, :] = piece[0:64, :]
        rows[12 * t : 12 * t + 16, :] = piece[64:80, :].astype(F32)
    held[256:304, :] = rows[0:48, :].astype(BF16)
    leaving = [fetch(held, out.at[g], sems.at[g]) for g in range(out.shape[0])]
    for copy in leaving:
        copy.wait()


def ring_copies(payload, groups):
    pieces = [payload]
    for dx in range(1, RING):
        pieces.append(lax.ppermute(payload, "x", [(x, (x + dx) % RING) for x in range(RING)]))
    lanes = payload.shape[1]
    return pl.pallas_call(
        ring_kernel,
        out_shape=jax.ShapeDtypeStruct((groups, 304, lanes), BF16),
        in_specs=[VMEM] * RING,
        out_specs=HBM,
        scratch_shapes=[
            pltpu.VMEM((64, lanes), F32),
            pltpu.VMEM((304, lanes), BF16),
            pltpu.SemaphoreType.DMA((groups,)),
        ],
        compiler_params=pltpu.CompilerParams(vmem_limit_bytes=16 * MIB),
        cost_estimate=pl.CostEstimate(flops=0, bytes_accessed=3 * MIB, transcendentals=0),
        name="ring_copies",
    )(*pieces)


def near_blocks(items, first, last, targets, row_of, charges_of, acc):
    def some(n, _):
        results = []
        for u in range(UNROLL):
            code = items[n * UNROLL + u]
            target = code >> 10
            source = code & 1023
            place = target & 63
            charge = charges_of(source)
            total = None
            for h in range(2):
                tiles = []
                wide = []
                for k in range(3):
                    row = jnp.broadcast_to(row_of(h, source, k), (16, 128))
                    wide.append(jnp.concatenate([row, row], axis=1).astype(BF16))
                for q in range(8):
                    square = None
                    for k in range(3):
                        off = targets[place, k, 16 * q : 16 * q + 16, :] - wide[k]
                        square = off * off + BF16(SOFTENING) if k == 0 else square + off * off
                    tiles.append(lax.rsqrt(square))
                values = jnp.concatenate(tiles, axis=0)
                values = jnp.concatenate([values[:, :128], values[:, 128:]], axis=0)
                part = dot_nt(charge[h], values)
                total = part if total is None else total + part
            results.append((target, total))
        for target, total in results:
            acc[target] += total
        return 0

    lax.fori_loop(first, last, some, 0)


def local_kernel(
    lists, counts, comps, charges, targets, ghost_items, ghost_start, near, table, acc, items
):
    leaves = charges.shape[0]
    store_rows(table, comps)

    def leaf_entries(leaf, ends):
        local_end, ghost_end = ends
        ghost_start[leaf] = ghost_end
        live_count = counts[leaf]
        items[local_end] = leaf * 1024 + leaf
        local_end = local_end + 1
        for j in range(16):
            slot = lists[j, leaf]
            live = j < live_count
            is_local = slot < 64
            items[local_end] = leaf * 1024 + slot
            ghost_items[ghost_end] = leaf * 1024 + slot - 64
            local_end = local_end + jnp.where(live & is_local, 1, 0)
            ghost_end = ghost_end + jnp.where(live & jnp.logical_not(is_local), 1, 0)
        return local_end, ghost_end

    local_end, ghost_end = lax.fori_loop(0, leaves, leaf_entries, (I32(0), I32(0)))
    for u in range(UNROLL):
        items[local_end + u] = 64 * 1024
        ghost_items[ghost_end + u] = 64 * 1024
    ghost_start[leaves] = ghost_end

    def spread(leaf, _):
        cols = [table[h, pl.ds(pl.multiple_of(8 * leaf, 8), 8), :].T for h in range(2)]
        for k in range(3):
            halves = [jnp.broadcast_to(cols[h][:, k : k + 1], (128, 128)) for h in range(2)]
            targets[leaf, k] = jnp.concatenate(halves, axis=1).astype(BF16)
        return 0

    lax.fori_loop(0, leaves, spread, 0, unroll=2)

    acc[...] = jnp.zeros_like(acc)
    near_blocks(
        items,
        0,
        (local_end + UNROLL - 1) // UNROLL,
        targets,
        lambda h, s, k: table[h, pl.ds(8 * s + k, 1), :],
        lambda s: [charges[s, :, 0:128], charges[s, :, 128:256]],
        acc,
    )
    near[...] = acc[0:leaves]


def local_near(lists, counts, comps, charges):
    leaves, rhs, points = charges.shape
    return pl.pallas_call(
        local_kernel,
        out_shape=(
            jax.ShapeDtypeStruct((leaves, 3, 128, points), BF16),
            jax.ShapeDtypeStruct((leaves * 16 + UNROLL,), I32),
            jax.ShapeDtypeStruct((leaves + 1,), I32),
            jax.ShapeDtypeStruct((leaves, rhs, points), F32),
        ),
        in_specs=[SMEM, SMEM, VMEM, VMEM],
        out_specs=(VMEM, SMEM, SMEM, VMEM),
        scratch_shapes=[
            pltpu.VMEM((2, leaves * 8, 128), F32),
            pltpu.VMEM((leaves + 1, rhs, points), F32),
            pltpu.SMEM((leaves * 17 + UNROLL,), I32),
        ],
        compiler_params=pltpu.CompilerParams(vmem_limit_bytes=VMEM_LIMIT),
        cost_estimate=pl.CostEstimate(
            flops=2 * 10**9, bytes_accessed=15 * MIB, transcendentals=8 * 10**6
        ),
        name="local_near",
    )(lists, counts, comps, charges)


PARTS = 4


def ghost_kernel(
    items_hbm,
    starts_hbm,
    ghosts_hbm,
    targets_hbm,
    start_hbm,
    near_hbm,
    ghosts,
    targets,
    table,
    acc,
    items,
    starts,
    sems,
):
    leaves = start_hbm.shape[0]
    part = leaves // PARTS
    senders = ghosts.shape[0] // PARTS

    def arrival(q):
        span = pl.ds(q * senders, senders)
        return pltpu.make_async_copy(ghosts_hbm.at[span], ghosts.at[span], sems.at[0, q])

    def piece(q):
        span = pl.ds(q * part, part)
        return pltpu.make_async_copy(targets_hbm.at[span], targets.at[span], sems.at[1, q])

    def result(q):
        span = pl.ds(q * part, part)
        return pltpu.make_async_copy(acc.at[span], near_hbm.at[span], sems.at[2, q])

    for q in range(PARTS):
        arrival(q).start()
    begin = fetch(start_hbm, acc.at[pl.ds(0, leaves)], sems.at[3, 0])
    listed = fetch(items_hbm, items, sems.at[3, 1])
    bounds = fetch(starts_hbm, starts, sems.at[3, 2])
    piece(0).start()
    acc[leaves] = jnp.zeros(acc.shape[1:], F32)

    def widen(e, _):
        rows = ghosts[e, 128:152, :].astype(F32)
        table[pl.ds(pl.multiple_of(24 * e, 8), 24), :] = rows
        return 0

    def arrived(q, _):
        arrival(q).wait()
        lax.fori_loop(0, senders, lambda n, _: widen(q * senders + n, _), 0, unroll=8)
        return 0

    lax.fori_loop(0, PARTS, arrived, 0)
    begin.wait()
    listed.wait()
    bounds.wait()
    for q in range(1, PARTS):
        piece(q).start()

    def charges_of(s):
        return [
            ghosts[s >> 2, pl.ds(pl.multiple_of(64 * h + 16 * (s & 3), 16), 16), :]
            for h in range(2)
        ]

    def run(q, _):
        piece(q).wait()
        end = starts[(q + 1) * part]
        last = jnp.where(q == PARTS - 1, (end + UNROLL - 1) // UNROLL, end // UNROLL)
        near_blocks(
            items,
            starts[q * part] // UNROLL,
            last,
            targets,
            lambda h, s, k: table[pl.ds(6 * s + 2 * k + h, 1), :],
            charges_of,
            acc,
        )
        return 0

    lax.fori_loop(0, PARTS, run, 0)
    for q in range(PARTS):
        result(q).start()
    for q in range(PARTS):
        result(q).wait()


def ghost_near(items, starts, ghosts, targets, start):
    leaves, rhs, points = start.shape
    devices = ghosts.shape[0]
    return pl.pallas_call(
        ghost_kernel,
        out_shape=jax.ShapeDtypeStruct(start.shape, F32),
        in_specs=[HBM, HBM, HBM, HBM, HBM],
        out_specs=HBM,
        scratch_shapes=[
            pltpu.VMEM(ghosts.shape, BF16),
            pltpu.VMEM(targets.shape, BF16),
            pltpu.VMEM((devices * 24, 128), F32),
            pltpu.VMEM((leaves + 1, rhs, points), F32),
            pltpu.SMEM(items.shape, I32),
            pltpu.SMEM(starts.shape, I32),
            pltpu.SemaphoreType.DMA((4, PARTS)),
        ],
        compiler_params=pltpu.CompilerParams(vmem_limit_bytes=VMEM_LIMIT),
        cost_estimate=pl.CostEstimate(
            flops=10**10, bytes_accessed=20 * MIB, transcendentals=4 * 10**7
        ),
        name="ghost_near",
    )(items, starts, ghosts, targets, start)


def finish_kernel(
    far,
    parents,
    skel,
    transfer_hbm,
    basis_hbm,
    near_hbm,
    out_hbm,
    out,
    transfer,
    basis,
    near,
    table,
    own,
    local,
    sems,
    *,
    scales,
):
    near_scale, far_scale = scales
    clusters, length = far.shape
    fetches = [
        fetch(source, target, sems.at[n])
        for n, (source, target) in enumerate(
            [
                (transfer_hbm, transfer),
                (basis_hbm, basis),
                (near_hbm, near),
            ]
        )
    ]

    def widen(e, _):
        table[pl.ds(pl.multiple_of(48 * e, 16), 48), :] = parents[e, 256:304, :].astype(F32)
        return 0

    lax.fori_loop(0, parents.shape[0], widen, 0, unroll=4)
    own[...] = jnp.zeros_like(own)
    for k in range(3):
        rows = skel[k].astype(F32)
        own[pl.ds(k, clusters, stride=8), :] = jnp.concatenate([rows, rows], axis=1)

    half = (lax.broadcasted_iota(I32, (16, 128), 1) >= 64).astype(I32)

    def coefficients(p, _):
        cols = own[pl.ds(pl.multiple_of(8 * p, 8), 8), :].T
        target = [
            jnp.broadcast_to(cols[0:64, k : k + 1], (64, 128)).astype(BF16) for k in range(3)
        ]
        target = [jnp.concatenate([t, t], axis=1) for t in target]
        total = jnp.zeros((16, 64), F32)
        for first in range(0, length, 2):
            moments = []
            rows = [[], [], []]
            for f in (first, first + 1):
                code = far[p, min(f, length - 1)]
                group, inner, wanted = code >> 8, code & 15, (code >> 4) & 1
                wanted = wanted if f < length else 2
                moment = parents[group, pl.ds(pl.multiple_of(16 * inner, 16), 16), :]
                moments.append(jnp.where(half == wanted, moment.astype(F32), F32(0.0)))
                for k in range(3):
                    row = table[pl.ds(48 * group + 3 * inner + k, 1), :]
                    rows[k].append(jnp.broadcast_to(row, (16, 128)))
            rows = [jnp.concatenate(r, axis=1).astype(BF16) for r in rows]
            tiles = []
            for q in range(4):
                square = None
                for k in range(3):
                    off = target[k][16 * q : 16 * q + 16, :] - rows[k]
                    square = off * off + BF16(SOFTENING) if k == 0 else square + off * off
                tiles.append(lax.rsqrt(square))
            moment = jnp.concatenate(moments, axis=1).astype(BF16)
            total = total + dot_nt(moment, jnp.concatenate(tiles, axis=0))
        local[p] = (far_scale * total).astype(BF16)
        return 0

    lax.fori_loop(0, clusters, coefficients, 0, unroll=4)

    for copy in fetches:
        copy.wait()
    block = own_blocks()

    def leaves_of(p):
        coef = local[p]
        coef = jnp.concatenate([coef, coef, coef, coef], axis=0)
        for quad in range(2):
            leaf = p * GROUP + 4 * quad
            child = dot_nt(coef, transfer[pl.ds(leaf, 4)].reshape(256, 64))
            child = jnp.where(block, child, F32(0.0)).astype(BF16)
            field = dot_nn(child, basis[pl.ds(leaf, 4)].reshape(256, 256))
            total = near_scale * near[pl.ds(leaf, 4)] + field.reshape(4, 16, 256)
            out[pl.ds(leaf, 4)] = total.astype(BF16)

    def half_of(n):
        span = pl.ds(n * 4 * GROUP, 4 * GROUP)
        return pltpu.make_async_copy(out.at[span], out_hbm.at[span], sems.at[3 + n])

    def half_leaves(n, _):
        for p in range(4):
            leaves_of(4 * n + p)
        half_of(n).start()
        return 0

    lax.fori_loop(0, 2, half_leaves, 0)
    for n in range(2):
        half_of(n).wait()


def finish(far, parents, skel, transfer, basis, near, scales):
    devices = parents.shape[0] * RING
    return pl.pallas_call(
        functools.partial(finish_kernel, scales=scales),
        out_shape=jax.ShapeDtypeStruct(near.shape, BF16),
        in_specs=[SMEM, VMEM, VMEM, HBM, HBM, HBM],
        out_specs=HBM,
        scratch_shapes=[
            pltpu.VMEM(near.shape, BF16),
            pltpu.VMEM(transfer.shape, BF16),
            pltpu.VMEM(basis.shape, BF16),
            pltpu.VMEM(near.shape, F32),
            pltpu.VMEM((devices * 12, 128), F32),
            pltpu.VMEM((64, 128), F32),
            pltpu.VMEM((far.shape[0], 16, 64), BF16),
            pltpu.SemaphoreType.DMA((3 + 2,)),
        ],
        compiler_params=pltpu.CompilerParams(vmem_limit_bytes=VMEM_LIMIT),
        cost_estimate=pl.CostEstimate(
            flops=10**8, bytes_accessed=8 * MIB, transcendentals=10**6
        ),
        name="finish",
    )(far, parents, skel, transfer, basis, near)


def body(
    coordinates,
    charges,
    leaf_basis,
    transfer,
    skeleton,
    send_plan,
    near_lists,
    near_count,
    far_lists,
):
    points = charges.shape[2]
    rank = leaf_basis.shape[1]
    devices = send_plan.shape[1]
    scales = (
        float(points * (near_lists.shape[1] + 1)) ** (-0.5),
        float(far_lists.shape[1] * rank) ** (-0.5),
    )
    comps = jnp.transpose(coordinates, (1, 0, 2))
    skel = jnp.transpose(skeleton, (1, 0, 2))
    packed = pack(jnp.transpose(send_plan, (0, 2, 1))[0], comps, charges)
    ghosts = lax.all_to_all(packed, AXES, split_axis=0, concat_axis=0, tiled=True)
    payload = parent_payload(charges, leaf_basis, transfer, skel)
    payload = ring_copies(payload, devices // RING)
    targets, items, starts, near = local_near(near_lists.T, near_count, comps, charges)
    apart = (lax.axis_index("x") - (far_lists >> 8)) & 3
    codes = ((far_lists >> 3) & 31) << 8 | (far_lists >> 2 & 1) << 4 | apart << 2 | far_lists & 3
    payload, ghosts, near, codes = lax.optimization_barrier((payload, ghosts, near, codes))
    parents = lax.all_to_all(payload, AXES[1:], split_axis=0, concat_axis=0, tiled=True)
    near = ghost_near(items, starts, ghosts, targets, near)
    return finish(codes, parents, skel, transfer, leaf_basis, near, scales)


def solution(mesh):
    grp, sub = mesh.shape["grp"], mesh.shape["sub"]
    sizes = (grp, RING, RING, sub // (RING * RING))
    apart = Mesh(mesh.devices.reshape(sizes), AXES)
    split3 = P(AXES, None, None)
    in_specs = (split3,) * 6 + (P(AXES, None), P(AXES), P(AXES, None))
    return jax.shard_map(body, mesh=apart, in_specs=in_specs, out_specs=split3, check_vma=False)
```
